32 devices in a mesh: gx: 8 (over z, y), gy: 4 (over x, core).
Axes of the slice: x: 2, y: 2, z: 4, core: 2. Of those that a mesh axis runs over, the one named last changes fastest.
Arguments:
- prec_pops: float32 [27, 32, 32, 256], P(None, 'gx', 'gy'), may hold values from 0 to 1, as said below
- main_pops: float32 [27, 64, 64, 256], P(None, 'gx', 'gy'), may hold values from 0 to 1, as said below
- cell_type: int32 [64, 64, 256], P('gx', 'gy'), may hold values from 0 to 2, as said below
- rates: float32 [27], replicated, may hold values from 0.7 to 1.8
Outputs:
- prec_next: float32 [27, 32, 32, 256], P(None, 'gx', 'gy')
- main_next: float32 [27, 64, 64, 256], P(None, 'gx', 'gy')
The draws below stay inside these ranges and needn't reach their ends.
Inputs may be any that keep to these rules, and one draw needn't show every extreme that they name: `prec_pops`: every population is positive; the populations of a cell sum to between 0.6 and 1.5. `main_pops`: every population is positive; the populations of a cell sum to between 0.6 and 1.5. `cell_type`: the lowest one to three cells of every column are solid (1); above them cells are fluid (0) or turbine disk (2).
All inputs are finite; a program needn't handle non-finite values.
Results may differ from the reference program's by a relative error of at most 0.000076.
Values sent between devices are 32-bit elements; how exact they have to be, the bound alone decides.
No kernel may reach another device: no remote copies, remote signals or barrier semaphores. Data moves between devices by JAX's collectives and lax.ppermute only.
A program may use at most 128 MiB of HBM per device.

```python
import math
import jax
import jax.numpy as jnp
import numpy as np
from jax import lax

NZ = 256
NXP = 32
NYP = 32
NXM = 64
NYM = 64


def draw_populations(key, extent_x, extent_y, depth):
    keys = jax.random.split(key, 5)
    shape = (extent_x, extent_y, depth)
    density = jax.random.uniform(keys[0], shape, jnp.float32, 0.9, 1.1)
    flow_x = jax.random.uniform(keys[1], shape, jnp.float32, -0.08, 0.08)
    flow_y = jax.random.uniform(keys[2], shape, jnp.float32, -0.08, 0.08)
    flow_z = jax.random.uniform(keys[3], shape, jnp.float32, -0.08, 0.08)
    speeds = jnp.asarray(np.array([[step_x, step_y, step_z] for step_x in (-1, 0, 1) for step_y in (-1, 0, 1) for step_z in (-1, 0, 1)]), jnp.float32)
    weights = jnp.prod(jnp.where(speeds == 0, 2.0 / 3.0, 1.0 / 6.0), axis=1)
    projected = speeds[:, 0, None, None, None] * flow_x[None] + speeds[:, 1, None, None, None] * flow_y[None] + speeds[:, 2, None, None, None] * flow_z[None]
    square = flow_x * flow_x + flow_y * flow_y + flow_z * flow_z
    equilibrium = weights[:, None, None, None] * density[None] * (1.0 + 3.0 * projected + 4.5 * projected * projected - 1.5 * square[None])
    noise = jax.random.uniform(keys[4], (27,) + shape, jnp.float32, -1.0, 1.0)
    return (equilibrium * (1.0 + 0.3 * noise)).astype(jnp.float32)


def draw_prec_pops(key, part):
    return draw_populations(jax.random.fold_in(key, 11), NXP, NYP, NZ)


def draw_main_pops(key, part):
    return draw_populations(jax.random.fold_in(key, 23), NXM, NYM, NZ)


def draw_cell_type(key, part):
    keys = jax.random.split(jax.random.fold_in(key, 37), 2)
    terrain = jax.random.randint(keys[0], (NXM, NYM, 1), 1, 4)
    height = lax.broadcasted_iota(jnp.int32, (NXM, NYM, NZ), 2)
    solid = height < terrain
    disk = jax.random.randint(keys[1], (NXM, NYM, NZ), 0, 12) == 0
    return jnp.where(solid, 1, jnp.where(disk, 2, 0)).astype(jnp.int32)


def setup_inputs(seed: int = 0) -> dict:
    key_of = jax.random.split(jax.random.key(seed), 5)
    prec_pops = draw_prec_pops(jax.random.fold_in(key_of[4], 71), 0)
    main_pops = draw_main_pops(jax.random.fold_in(key_of[4], 71), 0)
    cell_type = draw_cell_type(jax.random.fold_in(key_of[4], 71), 0)
    rates = jnp.clip(jnp.exp(jax.random.uniform(key_of[3], (27,), jnp.float32, math.log(0.7), math.log(1.8))), 0.7, 1.8)
    return dict(prec_pops=prec_pops, main_pops=main_pops, cell_type=cell_type, rates=rates)


thrust_coef = 0.75
highest = lax.Precision.HIGHEST


def lattice_speeds():
    return np.array([[step_x, step_y, step_z] for step_x in (-1, 0, 1) for step_y in (-1, 0, 1) for step_z in (-1, 0, 1)])


def lattice_weights():
    speeds = lattice_speeds()
    return np.prod(np.where(speeds == 0, 2.0 / 3.0, 1.0 / 6.0), axis=1)


def relax_matrix(rates):
    single = np.array([[1.0, 1.0, 1.0], [-1.0, 0.0, 1.0], [1.0, 0.0, 1.0]])
    inverse = np.array([[0.0, -0.5, 0.5], [1.0, 0.0, -1.0], [0.0, 0.5, 0.5]])
    moments = jnp.asarray(np.kron(np.kron(single, single), single), jnp.float32)
    inverse_full = jnp.asarray(np.kron(np.kron(inverse, inverse), inverse), jnp.float32)
    return jnp.dot(inverse_full * rates[None, :], moments, precision=highest)


def collide(populations, relaxer):
    cell_count = populations.shape[1] * populations.shape[2] * populations.shape[3]
    flattened = populations.reshape(27, cell_count)
    speeds = jnp.asarray(lattice_speeds().T, jnp.float32)
    weights = jnp.asarray(lattice_weights(), jnp.float32)
    density = jnp.sum(flattened, axis=0)
    velocity = jnp.dot(speeds, flattened, precision=highest) / density[None, :]
    projected = jnp.dot(speeds.T, velocity, precision=highest)
    square = jnp.sum(velocity * velocity, axis=0)
    equilibrium = weights[:, None] * density[None, :] * (1.0 + 3.0 * projected + 4.5 * projected * projected - 1.5 * square[None, :])
    relaxed = flattened - jnp.dot(relaxer, flattened - equilibrium, precision=highest)
    return flattened, relaxed, density, velocity


def apply_cells(flattened, relaxed, density, velocity, cell_type):
    flags = cell_type.reshape(-1)[None, :]
    speeds_x = jnp.asarray(lattice_speeds()[:, 0], jnp.float32)
    weights = jnp.asarray(lattice_weights(), jnp.float32)
    drag = -0.5 * thrust_coef * density * velocity[0] * jnp.abs(velocity[0])
    relaxed = relaxed + jnp.where(flags == 2, 3.0 * (weights * speeds_x)[:, None] * drag[None, :], 0.0)
    return jnp.where(flags == 1, flattened[::-1], relaxed)


def stream_pull(extended, relaxed):
    extent_x = relaxed.shape[1]
    extent_y = relaxed.shape[2]
    pulled = []
    for direction in range(27):
        step_x = direction // 9 - 1
        step_y = (direction // 3) % 3 - 1
        step_z = direction % 3 - 1
        shifted = extended[direction, 1 - step_x:1 - step_x + extent_x, 1 - step_y:1 - step_y + extent_y]
        if step_z == 1:
            shifted = jnp.concatenate([relaxed[26 - direction, :, :, :1], shifted[:, :, :-1]], axis=2)
        elif step_z == -1:
            shifted = jnp.concatenate([shifted[:, :, 1:], relaxed[26 - direction, :, :, -1:]], axis=2)
        pulled.append(shifted)
    return jnp.stack(pulled)


def extend_whole(relaxed, lower, upper):
    joined = jnp.concatenate([lower[:, None], relaxed, upper[:, None]], axis=1)
    return jnp.concatenate([joined[:, :, -1:], joined, joined[:, :, :1]], axis=2)


def reference(prec_pops, main_pops, cell_type, rates):
    relaxer = relax_matrix(rates)
    unused, prec_flat, prec_density, prec_velocity = collide(prec_pops, relaxer)
    prec_relaxed = prec_flat.reshape(prec_pops.shape)
    main_flat, main_relax, main_density, main_velocity = collide(main_pops, relaxer)
    main_relaxed = apply_cells(main_flat, main_relax, main_density, main_velocity, cell_type).reshape(main_pops.shape)
    prec_next = stream_pull(extend_whole(prec_relaxed, prec_relaxed[:, -1], prec_relaxed[:, 0]), prec_relaxed)
    inlet = jnp.concatenate([prec_relaxed[:, -1], prec_relaxed[:, -1]], axis=1)
    main_next = stream_pull(extend_whole(main_relaxed, inlet, main_relaxed[:, -1]), main_relaxed)
    return prec_next, main_next
```

```python
import jax
import jax.numpy as jnp
import numpy as np
from jax import lax
from jax.experimental import pallas as pl
from jax.experimental.pallas import tpu as pltpu
from jax.sharding import PartitionSpec as P

drag_scale = -0.5 * 0.75
vmem_bytes = 56 * 1024 * 1024
any_space = pl.BlockSpec(memory_space=pl.ANY)
vmem_space = pl.BlockSpec(memory_space=pltpu.VMEM)
smem_space = pl.BlockSpec(memory_space=pltpu.SMEM)


def swap_pairs(count, first):
    pairs = [(i, (i + 1) % count) for i in range(first, count, 2)]
    return [p for a, b in pairs for p in ((a, b), (b, a))]


def along_axes(values, stride, step):
    out = list(values)
    for start in range(27):
        if (start // stride) % 3 == 0:
            where = (start, start + stride, start + 2 * stride)
            for place, value in zip(where, step(*(values[i] for i in where))):
                out[place] = value
    return out


def to_moments(low, mid, high):
    outer = low + high
    return outer + mid, high - low, outer


def from_moments(zeroth, first, second):
    low, high = second - first, second + first
    return low, zeroth - (low + high), high


def digits(k):
    return k // 9, k // 3 % 3, k % 3


def moment_scales(rates_ref):
    keep, pull = [], []
    for k in range(27):
        ones = digits(k).count(1)
        twos = digits(k).count(2)
        half = 0.5 ** (ones + twos)
        third = 3.0 ** -(twos if ones else max(twos - 1, 0))
        rate = rates_ref[k]
        keep.append((1.0 - rate) * half)
        pull.append(rate * (half * third))
    return keep, pull


def relaxed_tile(pops, keep, pull, disk):
    m = pops
    for stride in (1, 3, 9):
        m = along_axes(m, stride, to_moments)
    density, flux = m[0], (m[9], m[3], m[1])
    inverse = 1.0 / density
    speed = [f * inverse for f in flux]
    third = density * (1.0 / 3.0)
    product = {(a, b): flux[a] * speed[b] for a in range(3) for b in range(a, 3)}
    drag = None
    if disk is not None:
        drag = jnp.where(disk, drag_scale * flux[0] * jnp.abs(speed[0]), 0.0)
    target = []
    for k in range(27):
        ones = [a for a in range(3) if digits(k)[a] == 1]
        twos = [a for a in range(3) if digits(k)[a] == 2]
        half = 0.5 ** (len(ones) + len(twos))
        if not ones and not twos:
            value = density
        elif len(ones) == 1 and not twos:
            value = m[k] * half
        elif len(ones) == 3:
            value = m[k] * keep[k]
        else:
            if len(ones) == 1:
                pulled = flux[ones[0]]
            elif len(ones) == 2:
                pulled = product[tuple(ones)]
            else:
                pulled = third
                for a in twos:
                    pulled = pulled + product[a, a]
            value = m[k] * keep[k] + pulled * pull[k]
        if drag is not None and ones == [0]:
            value = value + drag * (half * 3.0 ** -len(twos))
        target.append(value)
    for stride in (9, 3, 1):
        target = along_axes(target, stride, from_moments)
    return target


def collide_kernel(
    main_hbm, prec_hbm, cells_hbm, rates_ref,
    rel_main, rel_prec, send_a, send_b, send_c, send_d,
    main_in, prec_in, cells_in, side_low, side_high, in_sem, cell_sem, out_sem,
):
    extent_x, extent_y, depth = main_in.shape[1:]
    prec_x, prec_y = prec_in.shape[1:3]
    odd_x = lax.rem(lax.axis_index("gx"), 2)
    odd_y = lax.rem(lax.axis_index("gy"), 2)

    def fetch_main(x):
        return pltpu.make_async_copy(main_hbm.at[:, x], main_in.at[:, x], in_sem.at[x])

    def fetch_prec(x):
        return pltpu.make_async_copy(
            prec_hbm.at[:, x], prec_in.at[:, x], in_sem.at[extent_x + x]
        )

    fetch_cells = pltpu.make_async_copy(cells_hbm, cells_in, cell_sem)
    for x in range(prec_x):
        fetch_prec(x).start()
    fetch_cells.start()
    for x in range(extent_x):
        fetch_main(x).start()
    keep, pull = moment_scales(rates_ref)

    def prec_plane(x, carry):
        fetch_prec(x).wait()
        for y in range(0, prec_y, 8):
            for z in range(0, depth, 128):
                rows, lanes = pl.ds(y, 8), pl.ds(z, 128)
                pops = [prec_in[i, x, rows, lanes] for i in range(27)]
                for i, value in enumerate(relaxed_tile(pops, keep, pull, None)):
                    rel_prec[i, x, rows, lanes] = value
        return carry

    def main_plane(x, carry):
        fetch_main(x).wait()
        for y in range(0, extent_y, 8):
            for z in range(0, depth, 128):
                rows, lanes = pl.ds(y, 8), pl.ds(z, 128)
                kind = cells_in[x, rows, lanes]
                pops = [main_in[i, x, rows, lanes] for i in range(27)]
                for i, value in enumerate(relaxed_tile(pops, keep, pull, kind == 2)):
                    if z == 0:
                        value = jnp.where(kind == 1, main_in[26 - i, x, rows, lanes], value)
                    rel_main[i, x, rows, lanes] = value
        return carry

    lax.fori_loop(0, prec_x, prec_plane, 0)
    fetch_cells.wait()
    lax.fori_loop(0, extent_x, main_plane, 0)

    planes = extent_x + prec_x
    for pair in range(9):
        down, up = 9 * (pair // 3) + pair % 3, 9 * (pair // 3) + 6 + pair % 3
        for x in range(extent_x):
            place = pl.ds(pair * planes + x, 1)
            side_low[place, :] = rel_main[down, x, 0:1, :]
            side_high[place, :] = rel_main[up, x, extent_y - 1 : extent_y, :]
        for x in range(prec_x):
            place = pl.ds(pair * planes + extent_x + x, 1)
            side_low[place, :] = rel_prec[down, x, 0:1, :]
            side_high[place, :] = rel_prec[up, x, prec_y - 1 : prec_y, :]

    main_rows, prec_rows = pl.ds(0, extent_y), pl.ds(extent_y, prec_y)

    def faces(high_to, low_to):
        return (
            pltpu.make_async_copy(
                rel_main.at[18:27, extent_x - 1], high_to.at[:, main_rows], out_sem.at[0]
            ),
            pltpu.make_async_copy(
                rel_prec.at[18:27, prec_x - 1], high_to.at[:, prec_rows], out_sem.at[1]
            ),
            pltpu.make_async_copy(rel_main.at[0:9, 0], low_to.at[:, main_rows], out_sem.at[2]),
            pltpu.make_async_copy(rel_prec.at[0:9, 0], low_to.at[:, prec_rows], out_sem.at[3]),
        )

    def sides(high_to, low_to):
        return (
            pltpu.make_async_copy(side_high, high_to, out_sem.at[4]),
            pltpu.make_async_copy(side_low, low_to, out_sem.at[5]),
        )

    def both(odd, copies, one, other):
        @pl.when(odd == 0)
        def even_place():
            for copy in copies(one, other):
                copy.start()

        @pl.when(odd == 1)
        def odd_place():
            for copy in copies(other, one):
                copy.start()

    both(odd_x, faces, send_a, send_b)
    both(odd_y, sides, send_c, send_d)
    for copy in faces(send_a, send_b) + sides(send_c, send_d):
        copy.wait()


def corner_kernel(rel_prec, recv_c, recv_d, corner_a, corner_b, inlet_send, low_v, high_v, sem):
    prec_x, prec_y = rel_prec.shape[1:3]
    planes = recv_c.shape[0] // 9
    extent_x = planes - prec_x
    odd_x = lax.rem(lax.axis_index("gx"), 2)
    odd_y = lax.rem(lax.axis_index("gy"), 2)

    def from_sides(low_from, high_from):
        return (
            pltpu.make_async_copy(low_from, low_v, sem.at[0]),
            pltpu.make_async_copy(high_from, high_v, sem.at[1]),
        )

    @pl.when(odd_y == 0)
    def even_side():
        for copy in from_sides(recv_d, recv_c):
            copy.start()

    @pl.when(odd_y == 1)
    def odd_side():
        for copy in from_sides(recv_c, recv_d):
            copy.start()

    for copy in from_sides(recv_d, recv_c):
        copy.wait()

    def corners(ref, first, x_main, x_prec):
        for lattice, x in enumerate((x_main, extent_x + x_prec)):
            for step in range(3):
                place = pl.ds((first + step) * planes + x, 1)
                ref[lattice, step : step + 1, :] = low_v[place, :]
                ref[lattice, 3 + step : 4 + step, :] = high_v[place, :]

    corner_a[...] = jnp.zeros_like(corner_a)
    corner_b[...] = jnp.zeros_like(corner_b)

    @pl.when(odd_x == 0)
    def even_corner():
        corners(corner_a, 6, extent_x - 1, prec_x - 1)
        corners(corner_b, 0, 0, 0)

    @pl.when(odd_x == 1)
    def odd_corner():
        corners(corner_b, 6, extent_x - 1, prec_x - 1)
        corners(corner_a, 0, 0, 0)

    inlet_send[0:9] = rel_prec[18:27, prec_x - 1]
    inlet_send[9] = jnp.zeros(inlet_send.shape[1:], jnp.float32)

    @pl.when(odd_y == 0)
    def even_inlet():
        for step in range(3):
            place = pl.ds((6 + step) * planes + extent_x + prec_x - 1, 1)
            inlet_send[9, step : step + 1, :] = low_v[place, :]

    @pl.when(odd_y == 1)
    def odd_inlet():
        for step in range(3):
            place = pl.ds((6 + step) * planes + extent_x + prec_x - 1, 1)
            inlet_send[9, step : step + 1, :] = high_v[place, :]


def stream_kernel(
    rel_main, rel_prec, recv_a, recv_b, recv_c, recv_d, corner_a, corner_b, inlet_a, inlet_b,
    main_out, prec_out,
    main_v, prec_v, face_low, face_high, side_low, side_high, corner_low, corner_high, sem, out_sem,
):
    extent_x, extent_y, depth = rel_main.shape[1:]
    prec_x, prec_y = rel_prec.shape[1:3]
    planes = extent_x + prec_x
    place_x, place_y = lax.axis_index("gx"), lax.axis_index("gy")
    count_x, count_y = lax.axis_size("gx"), lax.axis_size("gy")
    odd_x, odd_y = lax.rem(place_x, 2), lax.rem(place_y, 2)

    def bring(low_from, high_from, low_to, high_to, first):
        return (
            pltpu.make_async_copy(low_from, low_to, sem.at[first]),
            pltpu.make_async_copy(high_from, high_to, sem.at[first + 1]),
        )

    groups = (
        (odd_x, recv_a, recv_b, face_low, face_high, 0),
        (odd_y, recv_c, recv_d, side_low, side_high, 2),
        (odd_x, corner_a, corner_b, corner_low, corner_high, 4),
    )
    for odd, one, other, low_to, high_to, first in groups:

        @pl.when(odd == 0)
        def even_place():
            for copy in bring(other, one, low_to, high_to, first):
                copy.start()

        @pl.when(odd == 1)
        def odd_place():
            for copy in bring(one, other, low_to, high_to, first):
                copy.start()

    for odd, one, other, low_to, high_to, first in groups:
        for copy in bring(other, one, low_to, high_to, first):
            copy.wait()

    def inlet(lower, upper):
        face_low[:, 0:prec_y] = lower[0:9]
        face_low[:, prec_y : 2 * prec_y] = upper[0:9]
        corner_low[0, 0:3] = lower[9, 0:3]
        corner_low[0, 3:6] = upper[9, 0:3]

    @pl.when((place_x == 0) & (place_y < count_y // 2))
    def near_inlet():
        inlet(inlet_a, inlet_b)

    @pl.when((place_x == 0) & (place_y >= count_y // 2))
    def far_inlet():
        inlet(inlet_b, inlet_a)

    @pl.when(place_x == count_x - 1)
    def outlet():
        face_high[:, 0:extent_y] = rel_main[0:9, extent_x - 1]
        for step in range(3):
            place = pl.ds(step * planes + extent_x - 1, 1)
            corner_high[0, step : step + 1, :] = side_low[place, :]
            corner_high[0, 3 + step : 4 + step, :] = side_high[place, :]

    def plane(x, rel, out, lattice, edge):
        size_x, size_y = rel.shape[1:3]
        start_y, start_x = (extent_y, extent_x) if lattice else (0, 0)
        row = lax.broadcasted_iota(jnp.int32, (size_y, depth), 0)
        lane = lax.broadcasted_iota(jnp.int32, (size_y, depth), 1)
        for i in range(27):
            step_x, step_y, step_z = (d - 1 for d in digits(i))
            pair = 3 * (step_x + 1) + step_z + 1
            source = x - step_x
            outside = None
            if edge == "first" and step_x == 1:
                outside = face_low, corner_low
            elif edge == "last" and step_x == -1:
                outside = face_high, corner_high
            if outside is not None:
                value = outside[0][3 * (step_y + 1) + step_z + 1, pl.ds(start_y, size_y), :]
            else:
                value = rel[i, source]
            if step_y:
                if outside is not None:
                    where = (0 if step_y == 1 else 3) + step_z + 1
                    halo = outside[1][lattice, where : where + 1, :]
                else:
                    side = side_low if step_y == 1 else side_high
                    halo = side[pl.ds(pair * planes + start_x + source, 1), :]
                value = pltpu.roll(value, 1 if step_y == 1 else size_y - 1, 0)
                value = jnp.where(row == (0 if step_y == 1 else size_y - 1), halo, value)
            if step_z:
                value = pltpu.roll(value, 1 if step_z == 1 else depth - 1, 1)
                value = jnp.where(
                    lane == (0 if step_z == 1 else depth - 1), rel[26 - i, x], value
                )
            out[i, x] = value

    def put(out_v, out_hbm, x, which):
        return pltpu.make_async_copy(out_v.at[:, x], out_hbm.at[:, x], out_sem.at[which])

    for rel, out_v, out_hbm, lattice in (
        (rel_main, main_v, main_out, 0),
        (rel_prec, prec_v, prec_out, 1),
    ):
        size_x = rel.shape[1]
        first = 0 if lattice == 0 else extent_x

        def inner(x, carry):
            plane(x, rel, out_v, lattice, "")
            put(out_v, out_hbm, x, first + x).start()
            return carry

        lax.fori_loop(1, size_x - 1, inner, 0)
        for x, edge in ((0, "first"), (size_x - 1, "last")):
            plane(x, rel, out_v, lattice, edge)
            put(out_v, out_hbm, x, first + x).start()
    for x in range(extent_x):
        put(main_v, main_out, x, x).wait()
    for x in range(prec_x):
        put(prec_v, prec_out, x, extent_x + x).wait()


def shards(prec_pops, main_pops, cell_type, rates):
    _, extent_x, extent_y, depth = main_pops.shape
    _, prec_x, prec_y, _ = prec_pops.shape
    count_x, count_y = lax.axis_size("gx"), lax.axis_size("gy")
    assert count_x % 2 == 0 and count_y % 2 == 0 and extent_y == 2 * prec_y
    planes = extent_x + prec_x
    f32 = jnp.float32
    face = jax.ShapeDtypeStruct((9, extent_y + prec_y, depth), f32)
    side = jax.ShapeDtypeStruct((9 * planes, depth), f32)
    params = pltpu.CompilerParams(vmem_limit_bytes=vmem_bytes)
    dma = pltpu.SemaphoreType.DMA
    main_rel, prec_rel, send_a, send_b, send_c, send_d = pl.pallas_call(
        collide_kernel,
        out_shape=(
            jax.ShapeDtypeStruct(main_pops.shape, f32),
            jax.ShapeDtypeStruct(prec_pops.shape, f32),
            face, face, side, side,
        ),
        in_specs=[any_space] * 3 + [smem_space],
        out_specs=(vmem_space, vmem_space) + (any_space,) * 4,
        scratch_shapes=[
            pltpu.VMEM(main_pops.shape, f32),
            pltpu.VMEM(prec_pops.shape, f32),
            pltpu.VMEM(cell_type.shape, jnp.int32),
            pltpu.VMEM(side.shape, f32),
            pltpu.VMEM(side.shape, f32),
            dma((planes,)), dma(()), dma((6,)),
        ],
        compiler_params=params,
        name="collide",
    )(main_pops, prec_pops, cell_type, rates)

    recv_c = lax.ppermute(send_c, "gy", swap_pairs(count_y, 0))
    recv_d = lax.ppermute(send_d, "gy", swap_pairs(count_y, 1))
    recv_a = lax.ppermute(send_a, "gx", swap_pairs(count_x, 0))
    recv_b = lax.ppermute(send_b, "gx", swap_pairs(count_x, 1))

    corner = jax.ShapeDtypeStruct((2, 8, depth), f32)
    corner_a, corner_b, inlet_send = pl.pallas_call(
        corner_kernel,
        out_shape=(corner, corner, jax.ShapeDtypeStruct((10, prec_y, depth), f32)),
        in_specs=[vmem_space, any_space, any_space],
        out_specs=(vmem_space,) * 3,
        scratch_shapes=[pltpu.VMEM(side.shape, f32), pltpu.VMEM(side.shape, f32), dma((2,))],
        compiler_params=params,
        name="corners",
    )(prec_rel, recv_c, recv_d)

    half = count_y // 2
    base = (count_x - 1) * count_y
    near = [(base + s, s // 2 + half * (s % 2)) for s in range(count_y)]
    far = [(base + s, s // 2 + half * (1 - s % 2)) for s in range(count_y)]
    corner_a = lax.ppermute(corner_a, "gx", swap_pairs(count_x, 0))
    corner_b = lax.ppermute(corner_b, "gx", swap_pairs(count_x, 1))
    inlet_a = lax.ppermute(inlet_send, ("gx", "gy"), near)
    inlet_b = lax.ppermute(inlet_send, ("gx", "gy"), far)

    main_next, prec_next = pl.pallas_call(
        stream_kernel,
        out_shape=(
            jax.ShapeDtypeStruct(main_pops.shape, f32),
            jax.ShapeDtypeStruct(prec_pops.shape, f32),
        ),
        in_specs=[vmem_space] * 2 + [any_space] * 6 + [vmem_space] * 2,
        out_specs=(any_space, any_space),
        scratch_shapes=[
            pltpu.VMEM(main_pops.shape, f32),
            pltpu.VMEM(prec_pops.shape, f32),
            pltpu.VMEM(face.shape, f32),
            pltpu.VMEM(face.shape, f32),
            pltpu.VMEM(side.shape, f32),
            pltpu.VMEM(side.shape, f32),
            pltpu.VMEM(corner.shape, f32),
            pltpu.VMEM(corner.shape, f32),
            dma((6,)), dma((planes,)),
        ],
        compiler_params=params,
        name="stream",
    )(
        main_rel, prec_rel, recv_a, recv_b, recv_c, recv_d,
        corner_a, corner_b, inlet_a, inlet_b,
    )
    return prec_next, main_next


def solution(mesh):
    placed = (P(None, "gx", "gy", None), P(None, "gx", "gy", None), P("gx", "gy", None), P())
    return jax.shard_map(
        shards,
        mesh=mesh,
        in_specs=placed,
        out_specs=(P(None, "gx", "gy", None), P(None, "gx", "gy", None)),
        check_vma=False,
    )
```

```python
import jax
import jax.numpy as jnp
import numpy as np
from jax import lax
from jax.experimental import pallas as pl
from jax.experimental.pallas import tpu as pltpu
from jax.sharding import PartitionSpec as P

drag_scale = -0.5 * 0.75
vmem_bytes = 20 * 1024 * 1024
any_space = pl.BlockSpec(memory_space=pltpu.HBM)
vmem_space = pl.BlockSpec(memory_space=pltpu.VMEM)
smem_space = pl.BlockSpec(memory_space=pltpu.SMEM)


def in_vmem(value):
    return pltpu.with_memory_space_constraint(value, pltpu.VMEM)


def in_hbm(value):
    return pltpu.with_memory_space_constraint(value, pltpu.HBM)


def swap_pairs(count, first):
    pairs = [(i, (i + 1) % count) for i in range(first, count, 2)]
    return [p for a, b in pairs for p in ((a, b), (b, a))]


def along_axes(values, stride, step):
    out = list(values)
    for start in range(27):
        if (start // stride) % 3 == 0:
            where = (start, start + stride, start + 2 * stride)
            for place, value in zip(where, step(*(values[i] for i in where))):
                out[place] = value
    return out


def to_moments(low, mid, high):
    outer = low + high
    return outer + mid, high - low, outer


def from_moments(zeroth, first, second):
    low, high = second - first, second + first
    return low, zeroth - (low + high), high


def digits(k):
    return k // 9, k // 3 % 3, k % 3


def moment_scales(rates_ref):
    keep, pull = [], []
    for k in range(27):
        ones = digits(k).count(1)
        twos = digits(k).count(2)
        half = 0.5 ** (ones + twos)
        third = 3.0 ** -(twos if ones else max(twos - 1, 0))
        rate = rates_ref[k]
        keep.append((1.0 - rate) * half)
        pull.append(rate * (half * third))
    return keep, pull


def relaxed_tile(pops, keep, pull, disk):
    m = pops
    for stride in (1, 3, 9):
        m = along_axes(m, stride, to_moments)
    density, flux = m[0], (m[9], m[3], m[1])
    inverse = 1.0 / density
    speed = [f * inverse for f in flux]
    third = density * (1.0 / 3.0)
    product = {(a, b): flux[a] * speed[b] for a in range(3) for b in range(a, 3)}
    drag = None
    if disk is not None:
        drag = jnp.where(disk, drag_scale * flux[0] * jnp.abs(speed[0]), 0.0)
    target = []
    for k in range(27):
        ones = [a for a in range(3) if digits(k)[a] == 1]
        twos = [a for a in range(3) if digits(k)[a] == 2]
        half = 0.5 ** (len(ones) + len(twos))
        if not ones and not twos:
            value = density
        elif len(ones) == 1 and not twos:
            value = m[k] * half
        elif len(ones) == 3:
            value = m[k] * keep[k]
        else:
            if len(ones) == 1:
                pulled = flux[ones[0]]
            elif len(ones) == 2:
                pulled = product[tuple(ones)]
            else:
                pulled = third
                for a in twos:
                    pulled = pulled + product[a, a]
            value = m[k] * keep[k] + pulled * pull[k]
        if drag is not None and ones == [0]:
            value = value + drag * (half * 3.0 ** -len(twos))
        target.append(value)
    for stride in (9, 3, 1):
        target = along_axes(target, stride, from_moments)
    return target


def collide_kernel(
    main_hbm, prec_hbm, cells_hbm, rates_ref,
    rel_main, rel_prec, send_a, send_b, send_c, send_d, inlet_send,
    main_in, prec_in, cells_in, in_sem, cell_sem,
):
    extent_x, extent_y, depth = main_in.shape[1:]
    prec_x, prec_y = prec_in.shape[1:3]
    odd_x = lax.rem(lax.axis_index("gx"), 2)
    odd_y = lax.rem(lax.axis_index("gy"), 2)

    def fetch_main(x):
        return pltpu.make_async_copy(main_hbm.at[:, x], main_in.at[:, x], in_sem.at[x])

    def fetch_prec(x):
        return pltpu.make_async_copy(
            prec_hbm.at[:, x], prec_in.at[:, x], in_sem.at[extent_x + x]
        )

    fetch_cells = pltpu.make_async_copy(cells_hbm, cells_in, cell_sem)
    for x in range(prec_x):
        fetch_prec(x).start()
    fetch_cells.start()
    for x in range(extent_x):
        fetch_main(x).start()
    keep, pull = moment_scales(rates_ref)

    def prec_plane(x, carry):
        fetch_prec(x).wait()
        for y in range(0, prec_y, 8):
            for z in range(0, depth, 128):
                rows, lanes = pl.ds(y, 8), pl.ds(z, 128)
                pops = [prec_in[i, x, rows, lanes] for i in range(27)]
                for i, value in enumerate(relaxed_tile(pops, keep, pull, None)):
                    rel_prec[i, x, rows, lanes] = value
        return carry

    def main_plane(x, carry):
        fetch_main(x).wait()
        for y in range(0, extent_y, 8):
            for z in range(0, depth, 128):
                rows, lanes = pl.ds(y, 8), pl.ds(z, 128)
                kind = cells_in[x, rows, lanes]
                pops = [main_in[i, x, rows, lanes] for i in range(27)]
                for i, value in enumerate(relaxed_tile(pops, keep, pull, kind == 2)):
                    if z == 0:
                        value = jnp.where(kind == 1, main_in[26 - i, x, rows, lanes], value)
                    rel_main[i, x, rows, lanes] = value
        return carry

    lax.fori_loop(0, prec_x, prec_plane, 0)
    fetch_cells.wait()
    lax.fori_loop(0, extent_x, main_plane, 0)

    def pick(odd, even_value, odd_value):
        return jnp.where(odd == 0, even_value, odd_value)

    planes = extent_x + prec_x
    for rel, first, size_x, size_y in (
        (rel_main, 0, extent_x, extent_y),
        (rel_prec, extent_y, prec_x, prec_y),
    ):
        for i in range(9):
            high, low = rel[18 + i, size_x - 1], rel[i, 0]
            send_a[i, first : first + size_y] = pick(odd_x, high, low)
            send_b[i, first : first + size_y] = pick(odd_x, low, high)
    inlet_send[...] = rel_prec[18:27, prec_x - 1]
    for pair in range(9):
        down, up = 9 * (pair // 3) + pair % 3, 9 * (pair // 3) + 6 + pair % 3
        for rel, first, size_x, size_y in (
            (rel_main, 0, extent_x, extent_y),
            (rel_prec, extent_x, prec_x, prec_y),
        ):
            for x in range(size_x):
                place = pl.ds(pair * planes + first + x, 1)
                low, high = rel[down, x, 0:1, :], rel[up, x, size_y - 1 : size_y, :]
                send_c[place, :] = pick(odd_y, high, low)
                send_d[place, :] = pick(odd_y, low, high)
    for step in range(3):
        place = pl.ds(9 * planes + step, 1)
        first, last = outlet_rows(rel_prec, step)
        send_c[place, :] = pick(odd_y, first, last)


def outlet_rows(rel_prec, step):
    prec_x, prec_y = rel_prec.shape[1:3]
    first = rel_prec[18 + step, prec_x - 1, 0:1, :]
    return first, rel_prec[24 + step, prec_x - 1, prec_y - 1 : prec_y, :]


def relay_kernel(send_d, recv_c, relayed_d):
    own = recv_c.shape[0] // 9 * 9
    relayed_d[0:own] = send_d[0:own]
    for step in range(recv_c.shape[0] - own):
        place = pl.ds(own + step, 1)
        relayed_d[place, :] = recv_c[place, :]


def own_rows_kernel(rel_prec, own_rows):
    own_rows[...] = jnp.zeros_like(own_rows)
    for step in range(3):
        first, last = outlet_rows(rel_prec, step)
        own_rows[step : step + 1, :] = last
        own_rows[3 + step : 4 + step, :] = first


def side_rows(recv_c, recv_d, odd_y, place):
    one, other = recv_c[pl.ds(place, 1), :], recv_d[pl.ds(place, 1), :]
    return jnp.where(odd_y == 0, other, one), jnp.where(odd_y == 0, one, other)


def corner_kernel(rel_prec, recv_c, recv_d, *rest):
    fetched, (corner_a, corner_b) = rest[:-2], rest[-2:]
    prec_x, prec_y = rel_prec.shape[1:3]
    planes = recv_c.shape[0] // 9
    extent_x = planes - prec_x
    place_x, place_y = lax.axis_index("gx"), lax.axis_index("gy")
    count_y = lax.axis_size("gy")
    odd_x, odd_y = lax.rem(place_x, 2), lax.rem(place_y, 2)
    at_last = place_x == lax.axis_size("gx") - 1

    def inlet_rows(step, low, high):
        if fetched:
            near = place_y < count_y // 2
            last = jnp.where(
                near, fetched[0][step : step + 1, :], fetched[1][step : step + 1, :]
            )
            first = jnp.where(
                near, fetched[2][3 + step : 4 + step, :], fetched[3][3 + step : 4 + step, :]
            )
            return last, first
        own_first, own_last = outlet_rows(rel_prec, step)
        beside = recv_c[pl.ds(9 * planes + step, 1), :]
        beyond = recv_d[pl.ds(9 * planes + step, 1), :]

        def choose(*options):
            value = options[0]
            for k in range(1, 4):
                value = jnp.where(place_y == k, options[k], value)
            return value

        return choose(low, own_last, beside, beyond), choose(beyond, beside, own_first, high)

    corner_a[...] = jnp.zeros_like(corner_a)
    corner_b[...] = jnp.zeros_like(corner_b)
    for step in range(3):
        outlet = side_rows(recv_c, recv_d, odd_y, (6 + step) * planes + planes - 1)
        inlet = inlet_rows(step, outlet[0], outlet[1])
        for lattice, (x_low, x_high) in enumerate(
            ((0, extent_x - 1), (extent_x, planes - 1))
        ):
            lows = side_rows(recv_c, recv_d, odd_y, step * planes + x_low)
            highs = side_rows(recv_c, recv_d, odd_y, (6 + step) * planes + x_high)
            for k in range(2):
                place = pl.ds(3 * k + step, 1)
                low, high = lows[k], highs[k]
                corner_a[lattice, place, :] = jnp.where(odd_x == 0, high, low)
                value = jnp.where(odd_x == 0, low, high)
                if lattice == 0:
                    value = jnp.where(at_last, inlet[k], value)
                corner_b[lattice, place, :] = value


def streamed(i, x, rel, source_rows, halo_row):
    size_y, depth = rel.shape[2:]
    _, step_y, step_z = (d - 1 for d in digits(i))
    value = source_rows
    if step_y:
        row = lax.broadcasted_iota(jnp.int32, (size_y, depth), 0)
        value = pltpu.roll(value, 1 if step_y == 1 else size_y - 1, 0)
        value = jnp.where(row == (0 if step_y == 1 else size_y - 1), halo_row, value)
    if step_z:
        lane = lax.broadcasted_iota(jnp.int32, (size_y, depth), 1)
        value = pltpu.roll(value, 1 if step_z == 1 else depth - 1, 1)
        value = jnp.where(lane == (0 if step_z == 1 else depth - 1), rel[26 - i, x], value)
    return value


def side_row(recv_c, recv_d, i, place, planes):
    step_x, step_y, step_z = (d - 1 for d in digits(i))
    odd = lax.rem(lax.axis_index("gy"), 2)
    where = pl.ds((3 * (step_x + 1) + step_z + 1) * planes + place, 1)
    from_low = odd if step_y == 1 else 1 - odd
    return jnp.where(from_low == 1, recv_c[where, :], recv_d[where, :])


def stream_kernel(
    rel_main, rel_prec, recv_c, recv_d, main_out, prec_out, main_v, prec_v, out_sem,
):
    planes = rel_main.shape[1] + rel_prec.shape[1]
    copies = []
    for rel, out_v, out_hbm, first in (
        (rel_main, main_v, main_out, 0),
        (rel_prec, prec_v, prec_out, rel_main.shape[1]),
    ):
        size_x = rel.shape[1]

        def emit(x, edges, rel=rel, out_v=out_v, first=first):
            for i in range(27):
                step_x, step_y, _ = (d - 1 for d in digits(i))
                if step_x in edges:
                    continue
                source = x - step_x
                halo = side_row(recv_c, recv_d, i, first + source, planes) if step_y else None
                out_v[i, x] = streamed(i, x, rel, rel[i, source], halo)

        def put(x, low, high, out_v=out_v, out_hbm=out_hbm, first=first):
            return pltpu.make_async_copy(
                out_v.at[low:high, x], out_hbm.at[low:high, x], out_sem.at[first + x]
            )

        def inner(x, carry, emit=emit, put=put):
            emit(x, ())
            put(x, 0, 27).start()
            return carry

        lax.fori_loop(1, size_x - 1, inner, 0)
        emit(0, (1,))
        copies.append(put(0, 0, 18))
        copies[-1].start()
        emit(size_x - 1, (-1,))
        copies.append(put(size_x - 1, 9, 27))
        copies[-1].start()
        copies.extend(put(x, 0, 27) for x in range(1, size_x - 1))
    for copy in copies:
        copy.wait()


def edge_kernel(
    rel_main, rel_prec, recv_a, recv_b, recv_c, recv_d, corner_a, corner_b, inlet_a, inlet_b,
    main_old, prec_old, main_out, prec_out, main_v, prec_v, out_sem,
):
    extent_x, extent_y, _ = rel_main.shape[1:]
    prec_x, prec_y = rel_prec.shape[1:3]
    planes = extent_x + prec_x
    place_x, place_y = lax.axis_index("gx"), lax.axis_index("gy")
    count_x, count_y = lax.axis_size("gx"), lax.axis_size("gy")
    odd_x = lax.rem(place_x, 2)
    at_first, at_last = place_x == 0, place_x == count_x - 1
    near = place_y < count_y // 2
    copies = []
    for rel, out_v, out_hbm, lattice in (
        (rel_prec, prec_v, prec_out, 1),
        (rel_main, main_v, main_out, 0),
    ):
        size_x, size_y = rel.shape[1:3]
        start_y = extent_y if lattice else 0
        for low_side in (True, False):
            x = 0 if low_side else size_x - 1
            from_one = odd_x if low_side else 1 - odd_x
            for part in range(9):
                i = part + (18 if low_side else 0)
                step_y, step_z = digits(i)[1] - 1, digits(i)[2] - 1
                rows = pl.ds(start_y, size_y)
                value = jnp.where(from_one == 1, recv_a[part, rows], recv_b[part, rows])
                halo = None
                if step_y:
                    where = pl.ds((0 if step_y == 1 else 3) + step_z + 1, 1)
                    halo = jnp.where(
                        from_one == 1, corner_a[lattice, where, :], corner_b[lattice, where, :]
                    )
                if not lattice and low_side:
                    lower = jnp.where(near, inlet_a[part], inlet_b[part])
                    upper = jnp.where(near, inlet_b[part], inlet_a[part])
                    whole = jnp.concatenate([lower, upper], axis=0)
                    value = jnp.where(at_first, whole, value)
                if not lattice and not low_side:
                    value = jnp.where(at_last, rel[i, size_x - 1], value)
                    if step_y:
                        row = side_row(recv_c, recv_d, i, size_x - 1, planes)
                        halo = jnp.where(at_last, row, halo)
                out_v[part, 0 if low_side else 1] = streamed(i, x, rel, value, halo)
            first = 18 if low_side else 0
            copy = pltpu.make_async_copy(
                out_v.at[:, 0 if low_side else 1],
                out_hbm.at[first : first + 9, x],
                out_sem.at[2 * lattice + (0 if low_side else 1)],
            )
            copy.start()
            copies.append(copy)
    for copy in copies:
        copy.wait()


def shards(prec_pops, main_pops, cell_type, rates):
    _, extent_x, extent_y, depth = main_pops.shape
    _, prec_x, prec_y, _ = prec_pops.shape
    count_x, count_y = lax.axis_size("gx"), lax.axis_size("gy")
    assert count_x % 2 == 0 and count_y % 2 == 0 and extent_y == 2 * prec_y
    planes = extent_x + prec_x
    f32 = jnp.float32
    face = (9, extent_y + prec_y, depth)
    side = (9 * planes + 3, depth)
    params = pltpu.CompilerParams(vmem_limit_bytes=vmem_bytes)
    dma = pltpu.SemaphoreType.DMA
    block = (9, prec_y, depth)
    main_rel, prec_rel, send_a, send_b, send_c, send_d, inlet_send = pl.pallas_call(
        collide_kernel,
        out_shape=tuple(
            pltpu.VMEM(shape, f32)
            for shape in (main_pops.shape, prec_pops.shape, face, face, side, side, block)
        ),
        in_specs=[any_space] * 3 + [smem_space],
        out_specs=(vmem_space,) * 7,
        scratch_shapes=[
            pltpu.VMEM(main_pops.shape, f32),
            pltpu.VMEM(prec_pops.shape, f32),
            pltpu.VMEM(cell_type.shape, jnp.int32),
            dma((planes,)), dma(()),
        ],
        compiler_params=params,
        name="collide",
    )(in_hbm(main_pops), in_hbm(prec_pops), in_hbm(cell_type), in_hbm(rates))
    main_rel, prec_rel = in_vmem(main_rel), in_vmem(prec_rel)

    half = count_y // 2
    base = (count_x - 1) * count_y
    near = [(base + s, s // 2 + half * (s % 2)) for s in range(count_y)]
    far = [(base + s, s // 2 + half * (1 - s % 2)) for s in range(count_y)]
    recv_a = in_vmem(lax.ppermute(send_a, "gx", swap_pairs(count_x, 0)))
    recv_b = in_vmem(lax.ppermute(send_b, "gx", swap_pairs(count_x, 1)))
    inlet_a = in_vmem(lax.ppermute(inlet_send, ("gx", "gy"), near))
    inlet_b = in_vmem(lax.ppermute(inlet_send, ("gx", "gy"), far))
    recv_c = in_vmem(lax.ppermute(send_c, "gy", swap_pairs(count_y, 0)))
    fetched = []
    if count_y == 4:
        send_d = pl.pallas_call(
            relay_kernel,
            out_shape=pltpu.VMEM(side, f32),
            in_specs=[vmem_space] * 2,
            out_specs=vmem_space,
            compiler_params=params,
            name="relay",
        )(in_vmem(send_d), recv_c)
    else:
        own_rows = pl.pallas_call(
            own_rows_kernel,
            out_shape=pltpu.VMEM((8, depth), f32),
            in_specs=[vmem_space],
            out_specs=vmem_space,
            compiler_params=params,
            name="outlet_rows",
        )(prec_rel)
        for shift in (-1, 2):
            for start in (0, half):
                pairs = [((2 * j + shift) % count_y, j) for j in range(start, start + half)]
                fetched.append(in_vmem(lax.ppermute(own_rows, "gy", pairs)))
    recv_d = in_vmem(lax.ppermute(send_d, "gy", swap_pairs(count_y, 1)))

    corner = (2, 8, depth)
    corner_a, corner_b = pl.pallas_call(
        corner_kernel,
        out_shape=(pltpu.VMEM(corner, f32),) * 2,
        in_specs=[vmem_space] * (3 + len(fetched)),
        out_specs=(vmem_space,) * 2,
        compiler_params=params,
        name="corners",
    )(prec_rel, recv_c, recv_d, *fetched)
    corner_a = in_vmem(lax.ppermute(corner_a, "gx", swap_pairs(count_x, 0)))
    corner_b = in_vmem(lax.ppermute(corner_b, "gx", swap_pairs(count_x, 1)))

    outs = (
        jax.ShapeDtypeStruct(main_pops.shape, f32),
        jax.ShapeDtypeStruct(prec_pops.shape, f32),
    )
    main_part, prec_part = pl.pallas_call(
        stream_kernel,
        out_shape=outs,
        in_specs=[vmem_space] * 4,
        out_specs=(any_space, any_space),
        scratch_shapes=[
            pltpu.VMEM(main_pops.shape, f32),
            pltpu.VMEM(prec_pops.shape, f32),
            dma((planes,)),
        ],
        compiler_params=params,
        name="stream",
    )(main_rel, prec_rel, recv_c, recv_d)
    main_next, prec_next = pl.pallas_call(
        edge_kernel,
        out_shape=outs,
        in_specs=[vmem_space] * 10 + [any_space] * 2,
        out_specs=(any_space, any_space),
        scratch_shapes=[
            pltpu.VMEM((9, 2, extent_y, depth), f32),
            pltpu.VMEM((9, 2, prec_y, depth), f32),
            dma((4,)),
        ],
        input_output_aliases={10: 0, 11: 1},
        compiler_params=params,
        name="edges",
    )(
        main_rel, prec_rel, recv_a, recv_b, recv_c, recv_d,
        corner_a, corner_b, inlet_a, inlet_b, main_part, prec_part,
    )
    return prec_next, main_next


def solution(mesh):
    placed = (P(None, "gx", "gy", None), P(None, "gx", "gy", None), P("gx", "gy", None), P())
    return jax.shard_map(
        shards,
        mesh=mesh,
        in_specs=placed,
        out_specs=(P(None, "gx", "gy", None), P(None, "gx", "gy", None)),
        check_vma=False,
    )
```

```python
import jax
import jax.numpy as jnp
import numpy as np
from jax import lax
from jax.experimental import pallas as pl
from jax.experimental.pallas import tpu as pltpu
from jax.sharding import PartitionSpec as P

drag_scale = -0.5 * 0.75
vmem_bytes = 20 * 1024 * 1024
any_space = pl.BlockSpec(memory_space=pltpu.HBM)
vmem_space = pl.BlockSpec(memory_space=pltpu.VMEM)
smem_space = pl.BlockSpec(memory_space=pltpu.SMEM)


def in_vmem(value):
    return pltpu.with_memory_space_constraint(value, pltpu.VMEM)


def in_hbm(value):
    return pltpu.with_memory_space_constraint(value, pltpu.HBM)


def swap_pairs(count, first):
    pairs = [(i, (i + 1) % count) for i in range(first, count, 2)]
    return [p for a, b in pairs for p in ((a, b), (b, a))]


def along_axes(values, stride, step):
    out = list(values)
    for start in range(27):
        if (start // stride) % 3 == 0:
            where = (start, start + stride, start + 2 * stride)
            for place, value in zip(where, step(*(values[i] for i in where))):
                out[place] = value
    return out


def to_moments(low, mid, high):
    outer = low + high
    return outer + mid, high - low, outer


def from_moments(zeroth, first, second):
    low, high = second - first, second + first
    return low, zeroth - (low + high), high


def digits(k):
    return k // 9, k // 3 % 3, k % 3


def moment_scales(rates_ref):
    keep, pull = [], []
    for k in range(27):
        ones = digits(k).count(1)
        twos = digits(k).count(2)
        half = 0.5 ** (ones + twos)
        third = 3.0 ** -(twos if ones else max(twos - 1, 0))
        rate = rates_ref[k]
        keep.append((1.0 - rate) * half)
        pull.append(rate * (half * third))
    return keep, pull


def relaxed_tile(pops, keep, pull, disk):
    m = pops
    for stride in (1, 3, 9):
        m = along_axes(m, stride, to_moments)
    density, flux = m[0], (m[9], m[3], m[1])
    inverse = 1.0 / density
    speed = [f * inverse for f in flux]
    third = density * (1.0 / 3.0)
    product = {(a, b): flux[a] * speed[b] for a in range(3) for b in range(a, 3)}
    drag = None
    if disk is not None:
        drag = jnp.where(disk, drag_scale * flux[0] * jnp.abs(speed[0]), 0.0)
    target = []
    for k in range(27):
        ones = [a for a in range(3) if digits(k)[a] == 1]
        twos = [a for a in range(3) if digits(k)[a] == 2]
        half = 0.5 ** (len(ones) + len(twos))
        if not ones and not twos:
            value = density
        elif len(ones) == 1 and not twos:
            value = m[k] * half
        elif len(ones) == 3:
            value = m[k] * keep[k]
        else:
            if len(ones) == 1:
                pulled = flux[ones[0]]
            elif len(ones) == 2:
                pulled = product[tuple(ones)]
            else:
                pulled = third
                for a in twos:
                    pulled = pulled + product[a, a]
            value = m[k] * keep[k] + pulled * pull[k]
        if drag is not None and ones == [0]:
            value = value + drag * (half * 3.0 ** -len(twos))
        target.append(value)
    for stride in (9, 3, 1):
        target = along_axes(target, stride, from_moments)
    return target


def collide_kernel(
    main_hbm, prec_hbm, cells_hbm, rates_ref,
    rel_main, rel_prec, send_a, send_b, send_c, send_d, inlet_send,
    main_in, prec_in, cells_in, in_sem, cell_sem,
):
    extent_x, extent_y, depth = main_in.shape[1:]
    prec_x, prec_y = prec_in.shape[1:3]
    odd_x = lax.rem(lax.axis_index("gx"), 2)
    odd_y = lax.rem(lax.axis_index("gy"), 2)

    def fetch_main(x):
        return pltpu.make_async_copy(main_hbm.at[:, x], main_in.at[:, x], in_sem.at[x])

    def fetch_prec(x):
        return pltpu.make_async_copy(
            prec_hbm.at[:, x], prec_in.at[:, x], in_sem.at[extent_x + x]
        )

    fetch_cells = pltpu.make_async_copy(cells_hbm, cells_in, cell_sem)
    for x in range(prec_x):
        fetch_prec(x).start()
    fetch_cells.start()
    for x in range(extent_x):
        fetch_main(x).start()
    keep, pull = moment_scales(rates_ref)

    def prec_plane(x, carry):
        fetch_prec(x).wait()
        for y in range(0, prec_y, 8):
            for z in range(0, depth, 128):
                rows, lanes = pl.ds(y, 8), pl.ds(z, 128)
                pops = [prec_in[i, x, rows, lanes] for i in range(27)]
                for i, value in enumerate(relaxed_tile(pops, keep, pull, None)):
                    rel_prec[i, x, rows, lanes] = value
        return carry

    def main_plane(x, carry):
        fetch_main(x).wait()
        for y in range(0, extent_y, 8):
            for z in range(0, depth, 128):
                rows, lanes = pl.ds(y, 8), pl.ds(z, 128)
                kind = cells_in[x, rows, lanes]
                pops = [main_in[i, x, rows, lanes] for i in range(27)]
                for i, value in enumerate(relaxed_tile(pops, keep, pull, kind == 2)):
                    if z == 0:
                        value = jnp.where(kind == 1, main_in[26 - i, x, rows, lanes], value)
                    rel_main[i, x, rows, lanes] = value
        return carry

    lax.fori_loop(0, prec_x, prec_plane, 0)
    fetch_cells.wait()
    lax.fori_loop(0, extent_x, main_plane, 0)

    def pick(odd, even_value, odd_value):
        return jnp.where(odd == 0, even_value, odd_value)

    planes = extent_x + prec_x
    for rel, first, size_x, size_y in (
        (rel_main, 0, extent_x, extent_y),
        (rel_prec, extent_y, prec_x, prec_y),
    ):
        for i in range(9):
            high, low = rel[18 + i, size_x - 1], rel[i, 0]
            send_a[i, first : first + size_y] = pick(odd_x, high, low)
            if first == 0:
                send_b[i] = pick(odd_x, low, high)
    inlet_send[...] = rel_prec[18:27, prec_x - 1]
    for pair in range(9):
        down, up = 9 * (pair // 3) + pair % 3, 9 * (pair // 3) + 6 + pair % 3
        for rel, first, size_x, size_y in (
            (rel_main, 0, extent_x, extent_y),
            (rel_prec, extent_x, prec_x, prec_y),
        ):
            for x in range(size_x):
                place = pl.ds(pair * planes + first + x, 1)
                low, high = rel[down, x, 0:1, :], rel[up, x, size_y - 1 : size_y, :]
                send_c[place, :] = pick(odd_y, high, low)
                send_d[place, :] = pick(odd_y, low, high)
    for step in range(3):
        place = pl.ds(9 * planes + step, 1)
        first, last = outlet_rows(rel_prec, step)
        send_c[place, :] = pick(odd_y, first, last)


def outlet_rows(rel_prec, step):
    prec_x, prec_y = rel_prec.shape[1:3]
    first = rel_prec[18 + step, prec_x - 1, 0:1, :]
    return first, rel_prec[24 + step, prec_x - 1, prec_y - 1 : prec_y, :]


def relay_kernel(send_d, recv_c, relayed_d):
    own = recv_c.shape[0] // 9 * 9
    relayed_d[0:own] = send_d[0:own]
    for step in range(recv_c.shape[0] - own):
        place = pl.ds(own + step, 1)
        relayed_d[place, :] = recv_c[place, :]


def own_rows_kernel(rel_prec, own_rows):
    own_rows[...] = jnp.zeros_like(own_rows)
    for step in range(3):
        first, last = outlet_rows(rel_prec, step)
        own_rows[step : step + 1, :] = last
        own_rows[3 + step : 4 + step, :] = first


def side_rows(recv_c, recv_d, odd_y, place):
    one, other = recv_c[pl.ds(place, 1), :], recv_d[pl.ds(place, 1), :]
    return jnp.where(odd_y == 0, other, one), jnp.where(odd_y == 0, one, other)


def corner_kernel(rel_prec, recv_a, recv_c, recv_d, *rest):
    fetched, (corner_a, corner_b) = rest[:-2], rest[-2:]
    prec_x, prec_y = rel_prec.shape[1:3]
    planes = recv_c.shape[0] // 9
    extent_x = planes - prec_x
    place_x, place_y = lax.axis_index("gx"), lax.axis_index("gy")
    count_y = lax.axis_size("gy")
    odd_x, odd_y = lax.rem(place_x, 2), lax.rem(place_y, 2)
    at_last = place_x == lax.axis_size("gx") - 1

    def inlet_rows(step, low, high):
        if fetched:
            near = place_y < count_y // 2
            last = jnp.where(
                near, fetched[0][step : step + 1, :], fetched[1][step : step + 1, :]
            )
            first = jnp.where(
                near, fetched[2][3 + step : 4 + step, :], fetched[3][3 + step : 4 + step, :]
            )
            return last, first
        own_first, own_last = outlet_rows(rel_prec, step)
        beside = recv_c[pl.ds(9 * planes + step, 1), :]
        beyond = recv_d[pl.ds(9 * planes + step, 1), :]

        def choose(*options):
            value = options[0]
            for k in range(1, 4):
                value = jnp.where(place_y == k, options[k], value)
            return value

        return choose(low, own_last, beside, beyond), choose(beyond, beside, own_first, high)

    corner_a[...] = jnp.zeros_like(corner_a)
    for i in range(9):
        corner_b[i] = jnp.where(odd_x == 0, rel_prec[i, 0], rel_prec[18 + i, prec_x - 1])
    corner_b[9:11] = jnp.zeros((2,) + corner_b.shape[1:], jnp.float32)
    for step in range(3):
        outlet = side_rows(recv_c, recv_d, odd_y, (6 + step) * planes + planes - 1)
        inlet = inlet_rows(step, outlet[0], outlet[1])
        for lattice, (x_low, x_high) in enumerate(
            ((0, extent_x - 1), (extent_x, planes - 1))
        ):
            lows = side_rows(recv_c, recv_d, odd_y, step * planes + x_low)
            highs = side_rows(recv_c, recv_d, odd_y, (6 + step) * planes + x_high)
            for k in range(2):
                place = pl.ds(3 * k + step, 1)
                low, high = lows[k], highs[k]
                corner_a[lattice, place, :] = jnp.where(odd_x == 0, high, low)
                value = jnp.where(odd_x == 0, low, high)
                if lattice == 0:
                    value = jnp.where(at_last, inlet[k], value)
                corner_b[9 + lattice, place, :] = value


def streamed(i, x, rel, source_rows, halo_row):
    size_y, depth = rel.shape[2:]
    _, step_y, step_z = (d - 1 for d in digits(i))
    value = source_rows
    if step_y:
        row = lax.broadcasted_iota(jnp.int32, (size_y, depth), 0)
        value = pltpu.roll(value, 1 if step_y == 1 else size_y - 1, 0)
        value = jnp.where(row == (0 if step_y == 1 else size_y - 1), halo_row, value)
    if step_z:
        lane = lax.broadcasted_iota(jnp.int32, (size_y, depth), 1)
        value = pltpu.roll(value, 1 if step_z == 1 else depth - 1, 1)
        value = jnp.where(lane == (0 if step_z == 1 else depth - 1), rel[26 - i, x], value)
    return value


def side_row(recv_c, recv_d, i, place, planes):
    step_x, step_y, step_z = (d - 1 for d in digits(i))
    odd = lax.rem(lax.axis_index("gy"), 2)
    where = pl.ds((3 * (step_x + 1) + step_z + 1) * planes + place, 1)
    from_low = odd if step_y == 1 else 1 - odd
    return jnp.where(from_low == 1, recv_c[where, :], recv_d[where, :])


def stream_kernel(
    rel_main, rel_prec, recv_c, recv_d, inlet_a, inlet_b,
    main_out, prec_out, main_v, prec_v, out_sem,
):
    planes = rel_main.shape[1] + rel_prec.shape[1]
    copies = []
    for rel, out_v, out_hbm, first in (
        (rel_main, main_v, main_out, 0),
        (rel_prec, prec_v, prec_out, rel_main.shape[1]),
    ):
        size_x = rel.shape[1]

        def emit(x, edges, rel=rel, out_v=out_v, first=first):
            for i in range(27):
                step_x, step_y, _ = (d - 1 for d in digits(i))
                if step_x in edges:
                    continue
                source = x - step_x
                halo = side_row(recv_c, recv_d, i, first + source, planes) if step_y else None
                out_v[i, x] = streamed(i, x, rel, rel[i, source], halo)

        def put(x, low, high, out_v=out_v, out_hbm=out_hbm, first=first):
            return pltpu.make_async_copy(
                out_v.at[low:high, x], out_hbm.at[low:high, x], out_sem.at[first + x]
            )

        def inner(x, carry, emit=emit, put=put):
            emit(x, ())
            put(x, 0, 27).start()
            return carry

        lax.fori_loop(1, size_x - 1, inner, 0)
        emit(0, (1,))
        copies.append(put(0, 0, 18))
        copies[-1].start()
        emit(size_x - 1, (-1,))
        copies.append(put(size_x - 1, 9, 27))
        copies[-1].start()
        copies.extend(put(x, 0, 27) for x in range(1, size_x - 1))
    for copy in copies:
        copy.wait()


def edge_kernel(
    rel_main, rel_prec, recv_a, recv_b, recv_c, recv_d, corner_a, corner_b, inlet_a, inlet_b,
    main_old, prec_old, main_out, prec_out, main_v, prec_v, out_sem,
):
    extent_x, extent_y, _ = rel_main.shape[1:]
    prec_x, prec_y = rel_prec.shape[1:3]
    planes = extent_x + prec_x
    place_x, place_y = lax.axis_index("gx"), lax.axis_index("gy")
    count_x, count_y = lax.axis_size("gx"), lax.axis_size("gy")
    odd_x = lax.rem(place_x, 2)
    at_first, at_last = place_x == 0, place_x == count_x - 1
    near = place_y < count_y // 2
    copies = []
    for rel, out_v, out_hbm, lattice in (
        (rel_prec, prec_v, prec_out, 1),
        (rel_main, main_v, main_out, 0),
    ):
        size_x, size_y = rel.shape[1:3]
        start_y = extent_y if lattice else 0
        for low_side in (True, False):
            x = 0 if low_side else size_x - 1
            from_one = odd_x if low_side else 1 - odd_x
            for part in range(9):
                i = part + (18 if low_side else 0)
                step_y, step_z = digits(i)[1] - 1, digits(i)[2] - 1
                rows = pl.ds(start_y, size_y)
                other = corner_b[part] if lattice else recv_b[part]
                value = jnp.where(from_one == 1, recv_a[part, rows], other)
                halo = None
                if step_y:
                    where = pl.ds((0 if step_y == 1 else 3) + step_z + 1, 1)
                    halo = jnp.where(
                        from_one == 1, corner_a[lattice, where, :], corner_b[9 + lattice, where, :]
                    )
                if not lattice and low_side:
                    lower = jnp.where(near, inlet_a[part], inlet_b[part])
                    upper = jnp.where(near, inlet_b[part], inlet_a[part])
                    whole = jnp.concatenate([lower, upper], axis=0)
                    value = jnp.where(at_first, whole, value)
                if not lattice and not low_side:
                    value = jnp.where(at_last, rel[i, size_x - 1], value)
                    if step_y:
                        row = side_row(recv_c, recv_d, i, size_x - 1, planes)
                        halo = jnp.where(at_last, row, halo)
                out_v[part, 0 if low_side else 1] = streamed(i, x, rel, value, halo)
            first = 18 if low_side else 0
            copy = pltpu.make_async_copy(
                out_v.at[:, 0 if low_side else 1],
                out_hbm.at[first : first + 9, x],
                out_sem.at[2 * lattice + (0 if low_side else 1)],
            )
            copy.start()
            copies.append(copy)
    for copy in copies:
        copy.wait()


def shards(prec_pops, main_pops, cell_type, rates):
    _, extent_x, extent_y, depth = main_pops.shape
    _, prec_x, prec_y, _ = prec_pops.shape
    count_x, count_y = lax.axis_size("gx"), lax.axis_size("gy")
    assert count_x % 2 == 0 and count_y % 2 == 0 and extent_y == 2 * prec_y
    planes = extent_x + prec_x
    f32 = jnp.float32
    face = (9, extent_y + prec_y, depth)
    side = (9 * planes + 3, depth)
    params = pltpu.CompilerParams(vmem_limit_bytes=vmem_bytes)
    dma = pltpu.SemaphoreType.DMA
    block = (9, prec_y, depth)
    main_rel, prec_rel, send_a, send_b, send_c, send_d, inlet_send = pl.pallas_call(
        collide_kernel,
        out_shape=tuple(
            pltpu.VMEM(shape, f32)
            for shape in (
                main_pops.shape, prec_pops.shape, face, (9, extent_y, depth), side, side, block
            )
        ),
        in_specs=[any_space] * 3 + [smem_space],
        out_specs=(vmem_space,) * 7,
        scratch_shapes=[
            pltpu.VMEM(main_pops.shape, f32),
            pltpu.VMEM(prec_pops.shape, f32),
            pltpu.VMEM(cell_type.shape, jnp.int32),
            dma((planes,)), dma(()),
        ],
        compiler_params=params,
        name="collide",
    )(in_hbm(main_pops), in_hbm(prec_pops), in_hbm(cell_type), in_hbm(rates))
    main_rel, prec_rel = in_vmem(main_rel), in_vmem(prec_rel)

    half = count_y // 2
    base = (count_x - 1) * count_y
    near = [(base + s, s // 2 + half * (s % 2)) for s in range(count_y)]
    far = [(base + s, s // 2 + half * (1 - s % 2)) for s in range(count_y)]
    recv_a = in_vmem(lax.ppermute(send_a, "gx", swap_pairs(count_x, 0)))
    across = [p for p in swap_pairs(count_x, 1) if abs(p[0] - p[1]) == 1]
    recv_b = in_vmem(lax.ppermute(send_b, "gx", across))
    inlet_a = in_vmem(lax.ppermute(inlet_send, ("gx", "gy"), near))
    inlet_b = in_vmem(lax.ppermute(inlet_send, ("gx", "gy"), far))
    recv_c = in_vmem(lax.ppermute(send_c, "gy", swap_pairs(count_y, 0)))
    fetched = []
    if count_y == 4:
        send_d = pl.pallas_call(
            relay_kernel,
            out_shape=pltpu.VMEM(side, f32),
            in_specs=[vmem_space] * 2,
            out_specs=vmem_space,
            compiler_params=params,
            name="relay",
        )(in_vmem(send_d), recv_c)
    else:
        own_rows = pl.pallas_call(
            own_rows_kernel,
            out_shape=pltpu.VMEM((8, depth), f32),
            in_specs=[vmem_space],
            out_specs=vmem_space,
            compiler_params=params,
            name="outlet_rows",
        )(prec_rel)
        for shift in (-1, 2):
            for start in (0, half):
                pairs = [((2 * j + shift) % count_y, j) for j in range(start, start + half)]
                fetched.append(in_vmem(lax.ppermute(own_rows, "gy", pairs)))
    recv_d = in_vmem(lax.ppermute(send_d, "gy", swap_pairs(count_y, 1)))

    corner = (2, 8, depth)
    corner_a, corner_b = pl.pallas_call(
        corner_kernel,
        out_shape=(pltpu.VMEM(corner, f32), pltpu.VMEM((11, prec_y, depth), f32)),
        in_specs=[vmem_space] * (4 + len(fetched)),
        out_specs=(vmem_space,) * 2,
        compiler_params=params,
        name="corners",
    )(prec_rel, recv_a, recv_c, recv_d, *fetched)
    corner_a = in_vmem(lax.ppermute(corner_a, "gx", swap_pairs(count_x, 0)))
    corner_b = in_vmem(lax.ppermute(corner_b, "gx", swap_pairs(count_x, 1)))

    outs = (
        jax.ShapeDtypeStruct(main_pops.shape, f32),
        jax.ShapeDtypeStruct(prec_pops.shape, f32),
    )
    main_part, prec_part = pl.pallas_call(
        stream_kernel,
        out_shape=outs,
        in_specs=[vmem_space] * 6,
        out_specs=(any_space, any_space),
        scratch_shapes=[
            pltpu.VMEM(main_pops.shape, f32),
            pltpu.VMEM(prec_pops.shape, f32),
            dma((planes,)),
        ],
        compiler_params=params,
        name="stream",
        cost_estimate=pl.CostEstimate(flops=10**9, bytes_accessed=1, transcendentals=0),
    )(main_rel, prec_rel, recv_c, recv_d, inlet_a, inlet_b)
    main_next, prec_next = pl.pallas_call(
        edge_kernel,
        out_shape=outs,
        in_specs=[vmem_space] * 10 + [any_space] * 2,
        out_specs=(any_space, any_space),
        scratch_shapes=[
            pltpu.VMEM((9, 2, extent_y, depth), f32),
            pltpu.VMEM((9, 2, prec_y, depth), f32),
            dma((4,)),
        ],
        input_output_aliases={10: 0, 11: 1},
        compiler_params=params,
        name="edges",
    )(
        main_rel, prec_rel, recv_a, recv_b, recv_c, recv_d,
        corner_a, corner_b, inlet_a, inlet_b, main_part, prec_part,
    )
    return prec_next, main_next


def solution(mesh):
    placed = (P(None, "gx", "gy", None), P(None, "gx", "gy", None), P("gx", "gy", None), P())
    return jax.shard_map(
        shards,
        mesh=mesh,
        in_specs=placed,
        out_specs=(P(None, "gx", "gy", None), P(None, "gx", "gy", None)),
        check_vma=False,
    )
```

```python
import functools

import jax
import jax.numpy as jnp
import numpy as np
from jax import lax
from jax.experimental import pallas as pl
from jax.experimental.pallas import tpu as pltpu
from jax.sharding import PartitionSpec as P

drag_scale = -0.5 * 0.75
vmem_bytes = 20 * 1024 * 1024
any_space = pl.BlockSpec(memory_space=pltpu.HBM)
vmem_space = pl.BlockSpec(memory_space=pltpu.VMEM)
smem_space = pl.BlockSpec(memory_space=pltpu.SMEM)


def in_vmem(value):
    return pltpu.with_memory_space_constraint(value, pltpu.VMEM)


def in_hbm(value):
    return pltpu.with_memory_space_constraint(value, pltpu.HBM)


def swap_pairs(count, first):
    pairs = [(i, (i + 1) % count) for i in range(first, count, 2)]
    return [p for a, b in pairs for p in ((a, b), (b, a))]


def along_axes(values, stride, step):
    out = list(values)
    for start in range(27):
        if (start // stride) % 3 == 0:
            where = (start, start + stride, start + 2 * stride)
            for place, value in zip(where, step(*(values[i] for i in where))):
                out[place] = value
    return out


def to_moments(low, mid, high):
    outer = low + high
    return outer + mid, high - low, outer


def from_moments(zeroth, first, second):
    low, high = second - first, second + first
    return low, zeroth - (low + high), high


def digits(k):
    return k // 9, k // 3 % 3, k % 3


def moment_scales(rates_ref):
    keep, pull = [], []
    for k in range(27):
        ones = digits(k).count(1)
        twos = digits(k).count(2)
        half = 0.5 ** (ones + twos)
        third = 3.0 ** -(twos if ones else max(twos - 1, 0))
        rate = rates_ref[k]
        keep.append((1.0 - rate) * half)
        pull.append(rate * (half * third))
    return keep, pull


def relaxed_tile(pops, keep, pull, disk):
    m = pops
    for stride in (1, 3, 9):
        m = along_axes(m, stride, to_moments)
    density, flux = m[0], (m[9], m[3], m[1])
    inverse = 1.0 / density
    speed = [f * inverse for f in flux]
    third = density * (1.0 / 3.0)
    product = {(a, b): flux[a] * speed[b] for a in range(3) for b in range(a, 3)}
    drag = None
    if disk is not None:
        drag = jnp.where(disk, drag_scale * flux[0] * jnp.abs(speed[0]), 0.0)
    target = []
    for k in range(27):
        ones = [a for a in range(3) if digits(k)[a] == 1]
        twos = [a for a in range(3) if digits(k)[a] == 2]
        half = 0.5 ** (len(ones) + len(twos))
        if not ones and not twos:
            value = density
        elif len(ones) == 1 and not twos:
            value = m[k] * half
        elif len(ones) == 3:
            value = m[k] * keep[k]
        else:
            if len(ones) == 1:
                pulled = flux[ones[0]]
            elif len(ones) == 2:
                pulled = product[tuple(ones)]
            else:
                pulled = third
                for a in twos:
                    pulled = pulled + product[a, a]
            value = m[k] * keep[k] + pulled * pull[k]
        if drag is not None and ones == [0]:
            value = value + drag * (half * 3.0 ** -len(twos))
        target.append(value)
    for stride in (9, 3, 1):
        target = along_axes(target, stride, from_moments)
    return target


def main_plane(main_in, cells_in, rel_main, keep, pull, slot, x):
    extent_y, depth = main_in.shape[2:]
    for y in range(0, extent_y, 8):
        for z in range(0, depth, 128):
            rows, lanes = pl.ds(y, 8), pl.ds(z, 128)
            kind = cells_in[x, rows, lanes]
            pops = [main_in[i, slot, rows, lanes] for i in range(27)]
            relaxed = relaxed_tile(pops, keep, pull, kind == 2)
            for i in range(27):
                value = relaxed[i]
                if z == 0:
                    value = jnp.where(kind == 1, pops[26 - i], value)
                rel_main[i, x, rows, lanes] = value


def border_kernel(
    main_hbm, prec_hbm, cells_hbm, rates_ref,
    cells_in, rel_main, rel_prec, send_a, send_b, send_c, send_d, inlet_send,
    outer_in, prec_in, main_low, main_high, prec_low, prec_high, plane_sem, row_sem,
):
    extent_x, extent_y, depth = rel_main.shape[1:]
    prec_x, prec_y = prec_in.shape[1:3]
    planes = extent_x + prec_x
    odd_x = lax.rem(lax.axis_index("gx"), 2)
    odd_y = lax.rem(lax.axis_index("gy"), 2)

    def pick(odd, even_value, odd_value):
        return jnp.where(odd == 0, even_value, odd_value)

    def fetch_prec(x):
        return pltpu.make_async_copy(prec_hbm.at[:, x], prec_in.at[:, x], plane_sem.at[3 + x])

    def fetch_outer(k):
        x = k * (extent_x - 1)
        return pltpu.make_async_copy(main_hbm.at[:, x], outer_in.at[:, k], plane_sem.at[k])

    fetch_cells = pltpu.make_async_copy(cells_hbm, cells_in, plane_sem.at[2])
    rows = []
    for hbm, low, high in ((main_hbm, main_low, main_high), (prec_hbm, prec_low, prec_high)):
        for x in range(hbm.shape[1]):
            for y, to in ((0, low), (hbm.shape[2] - 1, high)):
                rows.append(
                    pltpu.make_async_copy(
                        hbm.at[:, x, pl.ds(y, 1), :], to.at[:, pl.ds(x, 1), :],
                        row_sem.at[len(rows)],
                    )
                )
    for x in range(prec_x):
        fetch_prec(x).start()
    fetch_cells.start()
    for k in range(2):
        fetch_outer(k).start()
    for copy in rows:
        copy.start()
    keep, pull = moment_scales(rates_ref)

    def prec_plane(x, carry):
        fetch_prec(x).wait()
        for y in range(0, prec_y, 8):
            for z in range(0, depth, 128):
                rows, lanes = pl.ds(y, 8), pl.ds(z, 128)
                pops = [prec_in[i, x, rows, lanes] for i in range(27)]
                for i, value in enumerate(relaxed_tile(pops, keep, pull, None)):
                    rel_prec[i, x, rows, lanes] = value
        return carry

    def outer_plane(k, carry):
        fetch_outer(k).wait()
        main_plane(outer_in, cells_in, rel_main, keep, pull, k, k * (extent_x - 1))
        return carry

    lax.fori_loop(0, prec_x, prec_plane, 0)
    fetch_cells.wait()
    lax.fori_loop(0, 2, outer_plane, 0)

    for rel, first, size_x, size_y in (
        (rel_main, 0, extent_x, extent_y),
        (rel_prec, extent_y, prec_x, prec_y),
    ):
        for i in range(9):
            high, low = rel[18 + i, size_x - 1], rel[i, 0]
            send_a[i, first : first + size_y] = pick(odd_x, high, low)
            if first == 0:
                send_b[i] = pick(odd_x, low, high)
    inlet_send[...] = rel_prec[18:27, prec_x - 1]
    for step in range(3):
        place = pl.ds(9 * planes + step, 1)
        first, last = outlet_rows(rel_prec, step)
        send_c[place, :] = pick(odd_y, first, last)

    for copy in rows:
        copy.wait()
    for z in range(0, depth, 128):
        lanes = pl.ds(z, 128)
        for first, size_x, ends in (
            (0, extent_x, ((main_low, 0), (main_high, extent_y - 1))),
            (extent_x, prec_x, ((prec_low, None), (prec_high, None))),
        ):
            found = []
            for ref, y in ends:
                pops = [ref[i, :, lanes] for i in range(27)]
                kind = None if y is None else cells_in[:, y, lanes]
                disk = None if y is None else kind == 2
                relaxed = relaxed_tile(pops, keep, pull, disk)
                if y is not None and z == 0:
                    relaxed = [
                        jnp.where(kind == 1, pops[26 - i], relaxed[i]) for i in range(27)
                    ]
                found.append(relaxed)
            for pair in range(9):
                down, up = 9 * (pair // 3) + pair % 3, 9 * (pair // 3) + 6 + pair % 3
                place = pl.ds(pair * planes + first, size_x)
                low, high = found[0][down], found[1][up]
                send_c[place, lanes] = pick(odd_y, high, low)
                send_d[place, lanes] = pick(odd_y, low, high)


def inner_kernel(at_start, main_hbm, cells_in, rates_hbm, rel_old, *rest):
    rel_main, main_in, rates_ref, in_sem, rates_sem = rest[-6], *rest[-4:]

    @pl.when((lax.axis_index("gx") == 0) == at_start)
    def inner():
        def fetch(x):
            return pltpu.make_async_copy(main_hbm.at[:, x], main_in.at[:, x], in_sem.at[x])

        extent_x = main_in.shape[1]
        fetch_rates = pltpu.make_async_copy(rates_hbm, rates_ref, rates_sem)
        fetch_rates.start()
        for x in range(1, extent_x - 1):
            fetch(x).start()
        fetch_rates.wait()
        keep, pull = moment_scales(rates_ref)

        def plane(x, carry):
            fetch(x).wait()
            main_plane(main_in, cells_in, rel_main, keep, pull, x, x)
            return carry

        lax.fori_loop(1, extent_x - 1, plane, 0)


def outlet_rows(rel_prec, step):
    prec_x, prec_y = rel_prec.shape[1:3]
    first = rel_prec[18 + step, prec_x - 1, 0:1, :]
    return first, rel_prec[24 + step, prec_x - 1, prec_y - 1 : prec_y, :]


def relay_kernel(send_d, recv_c, relayed_d):
    own = recv_c.shape[0] // 9 * 9
    relayed_d[0:own] = send_d[0:own]
    for step in range(recv_c.shape[0] - own):
        place = pl.ds(own + step, 1)
        relayed_d[place, :] = recv_c[place, :]


def own_rows_kernel(rel_prec, own_rows):
    own_rows[...] = jnp.zeros_like(own_rows)
    for step in range(3):
        first, last = outlet_rows(rel_prec, step)
        own_rows[step : step + 1, :] = last
        own_rows[3 + step : 4 + step, :] = first


def side_rows(recv_c, recv_d, odd_y, place):
    one, other = recv_c[pl.ds(place, 1), :], recv_d[pl.ds(place, 1), :]
    return jnp.where(odd_y == 0, other, one), jnp.where(odd_y == 0, one, other)


def corner_kernel(rel_prec, recv_a, recv_c, recv_d, *rest):
    fetched, (corner_a, corner_b) = rest[:-2], rest[-2:]
    prec_x, prec_y = rel_prec.shape[1:3]
    planes = recv_c.shape[0] // 9
    extent_x = planes - prec_x
    place_x, place_y = lax.axis_index("gx"), lax.axis_index("gy")
    count_y = lax.axis_size("gy")
    odd_x, odd_y = lax.rem(place_x, 2), lax.rem(place_y, 2)
    at_last = place_x == lax.axis_size("gx") - 1

    def inlet_rows(step, low, high):
        if fetched:
            near = place_y < count_y // 2
            last = jnp.where(
                near, fetched[0][step : step + 1, :], fetched[1][step : step + 1, :]
            )
            first = jnp.where(
                near, fetched[2][3 + step : 4 + step, :], fetched[3][3 + step : 4 + step, :]
            )
            return last, first
        own_first, own_last = outlet_rows(rel_prec, step)
        beside = recv_c[pl.ds(9 * planes + step, 1), :]
        beyond = recv_d[pl.ds(9 * planes + step, 1), :]

        def choose(*options):
            value = options[0]
            for k in range(1, 4):
                value = jnp.where(place_y == k, options[k], value)
            return value

        return choose(low, own_last, beside, beyond), choose(beyond, beside, own_first, high)

    corner_a[...] = jnp.zeros_like(corner_a)
    for i in range(9):
        corner_b[i] = jnp.where(odd_x == 0, rel_prec[i, 0], rel_prec[18 + i, prec_x - 1])
    corner_b[9:11] = jnp.zeros((2,) + corner_b.shape[1:], jnp.float32)
    for step in range(3):
        outlet = side_rows(recv_c, recv_d, odd_y, (6 + step) * planes + planes - 1)
        inlet = inlet_rows(step, outlet[0], outlet[1])
        for lattice, (x_low, x_high) in enumerate(
            ((0, extent_x - 1), (extent_x, planes - 1))
        ):
            lows = side_rows(recv_c, recv_d, odd_y, step * planes + x_low)
            highs = side_rows(recv_c, recv_d, odd_y, (6 + step) * planes + x_high)
            for k in range(2):
                place = pl.ds(3 * k + step, 1)
                low, high = lows[k], highs[k]
                corner_a[lattice, place, :] = jnp.where(odd_x == 0, high, low)
                value = jnp.where(odd_x == 0, low, high)
                if lattice == 0:
                    value = jnp.where(at_last, inlet[k], value)
                corner_b[9 + lattice, place, :] = value


def streamed(i, x, rel, source_rows, halo_row):
    size_y, depth = rel.shape[2:]
    _, step_y, step_z = (d - 1 for d in digits(i))
    value = source_rows
    if step_y:
        row = lax.broadcasted_iota(jnp.int32, (size_y, depth), 0)
        value = pltpu.roll(value, 1 if step_y == 1 else size_y - 1, 0)
        value = jnp.where(row == (0 if step_y == 1 else size_y - 1), halo_row, value)
    if step_z:
        lane = lax.broadcasted_iota(jnp.int32, (size_y, depth), 1)
        value = pltpu.roll(value, 1 if step_z == 1 else depth - 1, 1)
        value = jnp.where(lane == (0 if step_z == 1 else depth - 1), rel[26 - i, x], value)
    return value


def side_row(recv_c, recv_d, i, place, planes):
    step_x, step_y, step_z = (d - 1 for d in digits(i))
    odd = lax.rem(lax.axis_index("gy"), 2)
    where = pl.ds((3 * (step_x + 1) + step_z + 1) * planes + place, 1)
    from_low = odd if step_y == 1 else 1 - odd
    return jnp.where(from_low == 1, recv_c[where, :], recv_d[where, :])


def stream_kernel(
    rel_main, rel_prec, recv_c, recv_d,
    main_out, prec_out, main_v, prec_v, out_sem,
):
    planes = rel_main.shape[1] + rel_prec.shape[1]
    copies = []
    for rel, out_v, out_hbm, first in (
        (rel_main, main_v, main_out, 0),
        (rel_prec, prec_v, prec_out, rel_main.shape[1]),
    ):
        size_x = rel.shape[1]

        def emit(x, edges, rel=rel, out_v=out_v, first=first):
            for i in range(27):
                step_x, step_y, _ = (d - 1 for d in digits(i))
                if step_x in edges:
                    continue
                source = x - step_x
                halo = side_row(recv_c, recv_d, i, first + source, planes) if step_y else None
                out_v[i, x] = streamed(i, x, rel, rel[i, source], halo)

        def put(x, low, high, out_v=out_v, out_hbm=out_hbm, first=first):
            return pltpu.make_async_copy(
                out_v.at[low:high, x], out_hbm.at[low:high, x], out_sem.at[first + x]
            )

        def inner(x, carry, emit=emit, put=put):
            emit(x, ())
            put(x, 0, 27).start()
            return carry

        lax.fori_loop(1, size_x - 1, inner, 0)
        emit(0, (1,))
        copies.append(put(0, 0, 18))
        copies[-1].start()
        emit(size_x - 1, (-1,))
        copies.append(put(size_x - 1, 9, 27))
        copies[-1].start()
        copies.extend(put(x, 0, 27) for x in range(1, size_x - 1))
    for copy in copies:
        copy.wait()


def edge_kernel(
    rel_main, rel_prec, recv_a, recv_b, recv_c, recv_d, corner_a, corner_b, inlet_a, inlet_b,
    main_old, prec_old, main_out, prec_out, main_v, prec_v, out_sem,
):
    extent_x, extent_y, _ = rel_main.shape[1:]
    prec_x, prec_y = rel_prec.shape[1:3]
    planes = extent_x + prec_x
    place_x, place_y = lax.axis_index("gx"), lax.axis_index("gy")
    count_x, count_y = lax.axis_size("gx"), lax.axis_size("gy")
    odd_x = lax.rem(place_x, 2)
    at_first, at_last = place_x == 0, place_x == count_x - 1
    near = place_y < count_y // 2
    copies = []
    for rel, out_v, out_hbm, lattice in (
        (rel_prec, prec_v, prec_out, 1),
        (rel_main, main_v, main_out, 0),
    ):
        size_x, size_y = rel.shape[1:3]
        start_y = extent_y if lattice else 0
        for low_side in (True, False):
            x = 0 if low_side else size_x - 1
            from_one = odd_x if low_side else 1 - odd_x
            for part in range(9):
                i = part + (18 if low_side else 0)
                step_y, step_z = digits(i)[1] - 1, digits(i)[2] - 1
                rows = pl.ds(start_y, size_y)
                other = corner_b[part] if lattice else recv_b[part]
                value = jnp.where(from_one == 1, recv_a[part, rows], other)
                halo = None
                if step_y:
                    where = pl.ds((0 if step_y == 1 else 3) + step_z + 1, 1)
                    halo = jnp.where(
                        from_one == 1, corner_a[lattice, where, :], corner_b[9 + lattice, where, :]
                    )
                if not lattice and low_side:
                    lower = jnp.where(near, inlet_a[part], inlet_b[part])
                    upper = jnp.where(near, inlet_b[part], inlet_a[part])
                    whole = jnp.concatenate([lower, upper], axis=0)
                    value = jnp.where(at_first, whole, value)
                if not lattice and not low_side:
                    value = jnp.where(at_last, rel[i, size_x - 1], value)
                    if step_y:
                        row = side_row(recv_c, recv_d, i, size_x - 1, planes)
                        halo = jnp.where(at_last, row, halo)
                out_v[part, 0 if low_side else 1] = streamed(i, x, rel, value, halo)
            first = 18 if low_side else 0
            copy = pltpu.make_async_copy(
                out_v.at[:, 0 if low_side else 1],
                out_hbm.at[first : first + 9, x],
                out_sem.at[2 * lattice + (0 if low_side else 1)],
            )
            copy.start()
            copies.append(copy)
    for copy in copies:
        copy.wait()


def shards(prec_pops, main_pops, cell_type, rates):
    _, extent_x, extent_y, depth = main_pops.shape
    _, prec_x, prec_y, _ = prec_pops.shape
    count_x, count_y = lax.axis_size("gx"), lax.axis_size("gy")
    assert count_x % 2 == 0 and count_y % 2 == 0 and extent_y == 2 * prec_y
    planes = extent_x + prec_x
    f32 = jnp.float32
    face = (9, extent_y + prec_y, depth)
    side = (9 * planes + 3, depth)
    params = pltpu.CompilerParams(vmem_limit_bytes=vmem_bytes)
    dma = pltpu.SemaphoreType.DMA
    block = (9, prec_y, depth)
    main_row, prec_row = (27, extent_x, depth), (27, prec_x, depth)
    cells_in, main_rel, prec_rel, send_a, send_b, send_c, send_d, inlet_send = pl.pallas_call(
        border_kernel,
        out_shape=(
            pltpu.VMEM(cell_type.shape, jnp.int32),
            *(
                pltpu.VMEM(shape, f32)
                for shape in (
                    main_pops.shape, prec_pops.shape,
                    face, (9, extent_y, depth), side, side, block,
                )
            ),
        ),
        in_specs=[any_space] * 3 + [smem_space],
        out_specs=(vmem_space,) * 8,
        scratch_shapes=[
            *(
                pltpu.VMEM(shape, f32)
                for shape in (
                    (27, 2, extent_y, depth), prec_pops.shape,
                    main_row, main_row, prec_row, prec_row,
                )
            ),
            dma((3 + prec_x,)), dma((2 * planes,)),
        ],
        compiler_params=params,
        name="border",
    )(in_hbm(main_pops), in_hbm(prec_pops), in_hbm(cell_type), in_hbm(rates))

    def inner(at_start, name, rel, held, *awaited):
        count = 4 + len(awaited)
        return pl.pallas_call(
            functools.partial(inner_kernel, at_start),
            out_shape=(pltpu.VMEM(rel.shape, f32), pltpu.VMEM(held.shape, f32)),
            in_specs=[any_space, vmem_space, any_space] + [vmem_space] * (count - 2),
            out_specs=(vmem_space,) * 2,
            scratch_shapes=[
                pltpu.VMEM(main_pops.shape, f32),
                pltpu.SMEM(rates.shape, f32),
                dma((extent_x,)), dma(()),
            ],
            input_output_aliases={3: 0, count: 1},
            compiler_params=params,
            name=name,
        )(in_hbm(main_pops), in_vmem(cells_in), in_hbm(rates), in_vmem(rel), *awaited, in_vmem(held))

    main_rel, send_b = inner(True, "inner_first", main_rel, send_b)
    prec_rel = in_vmem(prec_rel)

    half = count_y // 2
    base = (count_x - 1) * count_y
    near = [(base + s, s // 2 + half * (s % 2)) for s in range(count_y)]
    far = [(base + s, s // 2 + half * (1 - s % 2)) for s in range(count_y)]
    recv_a = in_vmem(lax.ppermute(send_a, "gx", swap_pairs(count_x, 0)))
    across = [p for p in swap_pairs(count_x, 1) if abs(p[0] - p[1]) == 1]
    recv_b = in_vmem(lax.ppermute(send_b, "gx", across))
    inlet_a = in_vmem(lax.ppermute(inlet_send, ("gx", "gy"), near))
    inlet_b = in_vmem(lax.ppermute(inlet_send, ("gx", "gy"), far))
    recv_c = in_vmem(lax.ppermute(send_c, "gy", swap_pairs(count_y, 0)))
    fetched = []
    if count_y == 4:
        send_d = pl.pallas_call(
            relay_kernel,
            out_shape=pltpu.VMEM(side, f32),
            in_specs=[vmem_space] * 2,
            out_specs=vmem_space,
            compiler_params=params,
            name="relay",
        )(in_vmem(send_d), recv_c)
    else:
        own_rows = pl.pallas_call(
            own_rows_kernel,
            out_shape=pltpu.VMEM((8, depth), f32),
            in_specs=[vmem_space],
            out_specs=vmem_space,
            compiler_params=params,
            name="outlet_rows",
        )(prec_rel)
        for shift in (-1, 2):
            for start in (0, half):
                pairs = [((2 * j + shift) % count_y, j) for j in range(start, start + half)]
                fetched.append(in_vmem(lax.ppermute(own_rows, "gy", pairs)))
    recv_d = in_vmem(lax.ppermute(send_d, "gy", swap_pairs(count_y, 1)))

    corner = (2, 8, depth)
    corner_a, corner_b = pl.pallas_call(
        corner_kernel,
        out_shape=(pltpu.VMEM(corner, f32), pltpu.VMEM((11, prec_y, depth), f32)),
        in_specs=[vmem_space] * (4 + len(fetched)),
        out_specs=(vmem_space,) * 2,
        compiler_params=params,
        name="corners",
    )(prec_rel, recv_a, recv_c, recv_d, *fetched)
    corner_a = in_vmem(lax.ppermute(corner_a, "gx", swap_pairs(count_x, 0)))
    corner_b = in_vmem(lax.ppermute(corner_b, "gx", swap_pairs(count_x, 1)))

    main_rel, prec_rel = inner(False, "inner_most", main_rel, prec_rel, inlet_a, inlet_b)
    main_rel, prec_rel = in_vmem(main_rel), in_vmem(prec_rel)
    outs = (
        jax.ShapeDtypeStruct(main_pops.shape, f32),
        jax.ShapeDtypeStruct(prec_pops.shape, f32),
    )
    main_part, prec_part = pl.pallas_call(
        stream_kernel,
        out_shape=outs,
        in_specs=[vmem_space] * 4,
        out_specs=(any_space, any_space),
        scratch_shapes=[
            pltpu.VMEM(main_pops.shape, f32),
            pltpu.VMEM(prec_pops.shape, f32),
            dma((planes,)),
        ],
        compiler_params=params,
        name="stream",
        cost_estimate=pl.CostEstimate(flops=10**9, bytes_accessed=1, transcendentals=0),
    )(main_rel, prec_rel, recv_c, recv_d)
    main_next, prec_next = pl.pallas_call(
        edge_kernel,
        out_shape=outs,
        in_specs=[vmem_space] * 10 + [any_space] * 2,
        out_specs=(any_space, any_space),
        scratch_shapes=[
            pltpu.VMEM((9, 2, extent_y, depth), f32),
            pltpu.VMEM((9, 2, prec_y, depth), f32),
            dma((4,)),
        ],
        input_output_aliases={10: 0, 11: 1},
        compiler_params=params,
        name="edges",
    )(
        main_rel, prec_rel, recv_a, recv_b, recv_c, recv_d,
        corner_a, corner_b, inlet_a, inlet_b, main_part, prec_part,
    )
    return prec_next, main_next


def solution(mesh):
    placed = (P(None, "gx", "gy", None), P(None, "gx", "gy", None), P("gx", "gy", None), P())
    return jax.shard_map(
        shards,
        mesh=mesh,
        in_specs=placed,
        out_specs=(P(None, "gx", "gy", None), P(None, "gx", "gy", None)),
        check_vma=False,
    )
```

```python
import functools

import jax
import jax.numpy as jnp
import numpy as np
from jax import lax
from jax.experimental import pallas as pl
from jax.experimental.pallas import tpu as pltpu
from jax.sharding import PartitionSpec as P

drag_scale = -0.5 * 0.75
vmem_bytes = 24 * 1024 * 1024
any_space = pl.BlockSpec(memory_space=pltpu.HBM)
vmem_space = pl.BlockSpec(memory_space=pltpu.VMEM)
smem_space = pl.BlockSpec(memory_space=pltpu.SMEM)


def in_vmem(value):
    return pltpu.with_memory_space_constraint(value, pltpu.VMEM)


def in_hbm(value):
    return pltpu.with_memory_space_constraint(value, pltpu.HBM)


def swap_pairs(count, first):
    pairs = [(i, (i + 1) % count) for i in range(first, count, 2)]
    return [p for a, b in pairs for p in ((a, b), (b, a))]


def along_axes(values, stride, step):
    out = list(values)
    for start in range(27):
        if (start // stride) % 3 == 0:
            where = (start, start + stride, start + 2 * stride)
            for place, value in zip(where, step(*(values[i] for i in where))):
                out[place] = value
    return out


def to_moments(low, mid, high):
    outer = low + high
    return outer + mid, high - low, outer


def from_moments(zeroth, first, second):
    low, high = second - first, second + first
    return low, zeroth - (low + high), high


def digits(k):
    return k // 9, k // 3 % 3, k % 3


def moment_scales(rates_ref):
    keep, pull = [], []
    for k in range(27):
        ones = digits(k).count(1)
        twos = digits(k).count(2)
        half = 0.5 ** (ones + twos)
        third = 3.0 ** -(twos if ones else max(twos - 1, 0))
        rate = rates_ref[k]
        keep.append((1.0 - rate) * half)
        pull.append(rate * (half * third))
    return keep, pull


def relaxed_tile(pops, keep, pull, disk):
    m = pops
    for stride in (1, 3, 9):
        m = along_axes(m, stride, to_moments)
    density, flux = m[0], (m[9], m[3], m[1])
    inverse = 1.0 / density
    speed = [f * inverse for f in flux]
    third = density * (1.0 / 3.0)
    product = {(a, b): flux[a] * speed[b] for a in range(3) for b in range(a, 3)}
    drag = None
    if disk is not None:
        drag = jnp.where(disk, drag_scale * flux[0] * jnp.abs(speed[0]), 0.0)
    target = []
    for k in range(27):
        ones = [a for a in range(3) if digits(k)[a] == 1]
        twos = [a for a in range(3) if digits(k)[a] == 2]
        half = 0.5 ** (len(ones) + len(twos))
        if not ones and not twos:
            value = density
        elif len(ones) == 1 and not twos:
            value = m[k] * half
        elif len(ones) == 3:
            value = m[k] * keep[k]
        else:
            if len(ones) == 1:
                pulled = flux[ones[0]]
            elif len(ones) == 2:
                pulled = product[tuple(ones)]
            else:
                pulled = third
                for a in twos:
                    pulled = pulled + product[a, a]
            value = m[k] * keep[k] + pulled * pull[k]
        if drag is not None and ones == [0]:
            value = value + drag * (half * 3.0 ** -len(twos))
        target.append(value)
    for stride in (9, 3, 1):
        target = along_axes(target, stride, from_moments)
    return target


def main_plane(main_in, cells_in, rel_main, keep, pull, slot, x):
    extent_y, depth = main_in.shape[2:]
    for y in range(0, extent_y, 8):
        for z in range(0, depth, 128):
            rows, lanes = pl.ds(y, 8), pl.ds(z, 128)
            kind = cells_in[x, rows, lanes]
            pops = [main_in[i, slot, rows, lanes] for i in range(27)]
            relaxed = relaxed_tile(pops, keep, pull, kind == 2)
            for i in range(27):
                value = relaxed[i]
                if z == 0:
                    value = jnp.where(kind == 1, pops[26 - i], value)
                rel_main[i, x, rows, lanes] = value


def border_kernel(
    main_hbm, prec_hbm, cells_hbm, rates_ref,
    cells_in, rel_main, rel_prec, send_a, send_b, send_c, send_d,
    outer_in, prec_in, main_low, main_high, prec_low, prec_high, plane_sem, row_sem,
):
    extent_x, extent_y, depth = rel_main.shape[1:]
    prec_x, prec_y = prec_in.shape[1:3]
    planes = extent_x + prec_x
    odd_x = lax.rem(lax.axis_index("gx"), 2)
    odd_y = lax.rem(lax.axis_index("gy"), 2)

    def pick(odd, even_value, odd_value):
        return jnp.where(odd == 0, even_value, odd_value)

    def fetch_prec(x):
        return pltpu.make_async_copy(prec_hbm.at[:, x], prec_in.at[:, x], plane_sem.at[3 + x])

    def fetch_outer(k):
        x = k * (extent_x - 1)
        return pltpu.make_async_copy(main_hbm.at[:, x], outer_in.at[:, k], plane_sem.at[k])

    fetch_cells = pltpu.make_async_copy(cells_hbm, cells_in, plane_sem.at[2])
    rows = []
    for hbm, low, high in ((main_hbm, main_low, main_high), (prec_hbm, prec_low, prec_high)):
        for x in range(hbm.shape[1]):
            for y, to in ((0, low), (hbm.shape[2] - 1, high)):
                rows.append(
                    pltpu.make_async_copy(
                        hbm.at[:, x, pl.ds(y, 1), :], to.at[:, pl.ds(x, 1), :],
                        row_sem.at[len(rows)],
                    )
                )
    for x in range(prec_x):
        fetch_prec(x).start()
    fetch_cells.start()
    for k in range(2):
        fetch_outer(k).start()
    for copy in rows:
        copy.start()
    keep, pull = moment_scales(rates_ref)

    def prec_plane(x, carry):
        fetch_prec(x).wait()
        for y in range(0, prec_y, 8):
            for z in range(0, depth, 128):
                rows, lanes = pl.ds(y, 8), pl.ds(z, 128)
                pops = [prec_in[i, x, rows, lanes] for i in range(27)]
                for i, value in enumerate(relaxed_tile(pops, keep, pull, None)):
                    rel_prec[i, x, rows, lanes] = value
        return carry

    def outer_plane(k, carry):
        fetch_outer(k).wait()
        main_plane(outer_in, cells_in, rel_main, keep, pull, k, k * (extent_x - 1))
        return carry

    lax.fori_loop(0, prec_x, prec_plane, 0)
    fetch_cells.wait()
    lax.fori_loop(0, 2, outer_plane, 0)

    for rel, first, size_x, size_y in (
        (rel_main, 0, extent_x, extent_y),
        (rel_prec, extent_y, prec_x, prec_y),
    ):
        for i in range(9):
            high, low = rel[18 + i, size_x - 1], rel[i, 0]
            send_a[i, first : first + size_y] = pick(odd_x, high, low)
            if first == 0:
                send_b[i] = pick(odd_x, low, high)
    for i in range(9):
        send_c[pl.ds(9 * planes + 4 + i * prec_y, prec_y), :] = rel_prec[18 + i, prec_x - 1]
    for step in range(3):
        place = pl.ds(9 * planes + step, 1)
        first, last = outlet_rows(rel_prec, step)
        send_c[place, :] = pick(odd_y, first, last)

    for copy in rows:
        copy.wait()
    for z in range(0, depth, 128):
        lanes = pl.ds(z, 128)
        for first, size_x, ends in (
            (0, extent_x, ((main_low, 0), (main_high, extent_y - 1))),
            (extent_x, prec_x, ((prec_low, None), (prec_high, None))),
        ):
            found = []
            for ref, y in ends:
                pops = [ref[i, :, lanes] for i in range(27)]
                kind = None if y is None else cells_in[:, y, lanes]
                disk = None if y is None else kind == 2
                relaxed = relaxed_tile(pops, keep, pull, disk)
                if y is not None and z == 0:
                    relaxed = [
                        jnp.where(kind == 1, pops[26 - i], relaxed[i]) for i in range(27)
                    ]
                found.append(relaxed)
            for pair in range(9):
                down, up = 9 * (pair // 3) + pair % 3, 9 * (pair // 3) + 6 + pair % 3
                place = pl.ds(pair * planes + first, size_x)
                low, high = found[0][down], found[1][up]
                send_c[place, lanes] = pick(odd_y, high, low)
                send_d[place, lanes] = pick(odd_y, low, high)


def inner_planes(
    main_hbm, cells_in, rates_hbm, rel_main, main_in, rates_ref, in_sem, rates_sem
):
    def fetch(x):
        return pltpu.make_async_copy(main_hbm.at[:, x], main_in.at[:, x], in_sem.at[x])

    extent_x = main_in.shape[1]
    fetch_rates = pltpu.make_async_copy(rates_hbm, rates_ref, rates_sem)
    fetch_rates.start()
    for x in range(1, extent_x - 1):
        fetch(x).start()
    fetch_rates.wait()
    keep, pull = moment_scales(rates_ref)

    def plane(x, carry):
        fetch(x).wait()
        main_plane(main_in, cells_in, rel_main, keep, pull, x, x)
        return carry

    lax.fori_loop(1, extent_x - 1, plane, 0)


def first_kernel(
    main_hbm, cells_in, rates_hbm, rel_old, held_old,
    rel_main, held, main_in, rates_ref, in_sem, rates_sem,
):
    @pl.when(lax.axis_index("gx") == 0)
    def inner():
        inner_planes(
            main_hbm, cells_in, rates_hbm, rel_main, main_in, rates_ref, in_sem, rates_sem
        )


def outlet_rows(rel_prec, step):
    prec_x, prec_y = rel_prec.shape[1:3]
    first = rel_prec[18 + step, prec_x - 1, 0:1, :]
    return first, rel_prec[24 + step, prec_x - 1, prec_y - 1 : prec_y, :]


def relay_kernel(rel_prec, send_d, recv_c, relayed_d, pair_send):
    prec_x, prec_y = rel_prec.shape[1:3]
    own = send_d.shape[0] // 9 * 9
    relayed_d[0:own] = send_d[0:own]
    for step in range(send_d.shape[0] - own):
        place = pl.ds(own + step, 1)
        relayed_d[place, :] = recv_c[place, :]
    odd_y = lax.rem(lax.axis_index("gy"), 2)
    for i in range(9):
        mine = rel_prec[18 + i, prec_x - 1]
        other = recv_c[pl.ds(own + 4 + i * prec_y, prec_y), :]
        pair_send[0, i] = jnp.where(odd_y == 0, mine, other)
        pair_send[1, i] = jnp.where(odd_y == 0, other, mine)


def own_rows_kernel(rel_prec, own_rows):
    own_rows[...] = jnp.zeros_like(own_rows)
    for step in range(3):
        first, last = outlet_rows(rel_prec, step)
        own_rows[step : step + 1, :] = last
        own_rows[3 + step : 4 + step, :] = first


def side_rows(recv_c, recv_d, odd_y, place):
    one, other = recv_c[pl.ds(place, 1), :], recv_d[pl.ds(place, 1), :]
    return jnp.where(odd_y == 0, other, one), jnp.where(odd_y == 0, one, other)


def corner_kernel(rel_prec, recv_c, recv_d, *rest):
    fetched, (corner_a, corner_b) = rest[:-2], rest[-2:]
    prec_x, prec_y = rel_prec.shape[1:3]
    planes = recv_d.shape[0] // 9
    extent_x = planes - prec_x
    place_x, place_y = lax.axis_index("gx"), lax.axis_index("gy")
    count_y = lax.axis_size("gy")
    odd_x, odd_y = lax.rem(place_x, 2), lax.rem(place_y, 2)
    at_last = place_x == lax.axis_size("gx") - 1

    def inlet_rows(step, low, high):
        if fetched:
            near = place_y < count_y // 2
            last = jnp.where(
                near, fetched[0][step : step + 1, :], fetched[1][step : step + 1, :]
            )
            first = jnp.where(
                near, fetched[2][3 + step : 4 + step, :], fetched[3][3 + step : 4 + step, :]
            )
            return last, first
        own_first, own_last = outlet_rows(rel_prec, step)
        beside = recv_c[pl.ds(9 * planes + step, 1), :]
        beyond = recv_d[pl.ds(9 * planes + step, 1), :]

        def choose(*options):
            value = options[0]
            for k in range(1, 4):
                value = jnp.where(place_y == k, options[k], value)
            return value

        return choose(low, own_last, beside, beyond), choose(beyond, beside, own_first, high)

    corner_a[...] = jnp.zeros_like(corner_a)
    for i in range(9):
        corner_b[i] = jnp.where(odd_x == 0, rel_prec[i, 0], rel_prec[18 + i, prec_x - 1])
    corner_b[9:11] = jnp.zeros((2,) + corner_b.shape[1:], jnp.float32)
    for step in range(3):
        outlet = side_rows(recv_c, recv_d, odd_y, (6 + step) * planes + planes - 1)
        inlet = inlet_rows(step, outlet[0], outlet[1])
        for lattice, (x_low, x_high) in enumerate(
            ((0, extent_x - 1), (extent_x, planes - 1))
        ):
            lows = side_rows(recv_c, recv_d, odd_y, step * planes + x_low)
            highs = side_rows(recv_c, recv_d, odd_y, (6 + step) * planes + x_high)
            for k in range(2):
                place = pl.ds(3 * k + step, 1)
                low, high = lows[k], highs[k]
                corner_a[lattice, place, :] = jnp.where(odd_x == 0, high, low)
                value = jnp.where(odd_x == 0, low, high)
                if lattice == 0:
                    value = jnp.where(at_last, inlet[k], value)
                corner_b[9 + lattice, place, :] = value


def streamed(i, x, rel, source_rows, halo_row):
    size_y, depth = rel.shape[2:]
    _, step_y, step_z = (d - 1 for d in digits(i))
    value = source_rows
    if step_y:
        row = lax.broadcasted_iota(jnp.int32, (size_y, depth), 0)
        value = pltpu.roll(value, 1 if step_y == 1 else size_y - 1, 0)
        value = jnp.where(row == (0 if step_y == 1 else size_y - 1), halo_row, value)
    if step_z:
        lane = lax.broadcasted_iota(jnp.int32, (size_y, depth), 1)
        value = pltpu.roll(value, 1 if step_z == 1 else depth - 1, 1)
        value = jnp.where(lane == (0 if step_z == 1 else depth - 1), rel[26 - i, x], value)
    return value


def side_row(recv_c, recv_d, i, place, planes):
    step_x, step_y, step_z = (d - 1 for d in digits(i))
    odd = lax.rem(lax.axis_index("gy"), 2)
    where = pl.ds((3 * (step_x + 1) + step_z + 1) * planes + place, 1)
    from_low = odd if step_y == 1 else 1 - odd
    return jnp.where(from_low == 1, recv_c[where, :], recv_d[where, :])


def stream_planes(
    rel_main, rel_prec, recv_c, recv_d, main_out, prec_out, main_v, prec_v, out_sem,
):
    planes = rel_main.shape[1] + rel_prec.shape[1]
    copies = []
    for rel, out_v, out_hbm, first in (
        (rel_main, main_v, main_out, 0),
        (rel_prec, prec_v, prec_out, rel_main.shape[1]),
    ):
        size_x = rel.shape[1]

        def emit(x, edges, rel=rel, out_v=out_v, first=first):
            for i in range(27):
                step_x, step_y, _ = (d - 1 for d in digits(i))
                if step_x in edges:
                    continue
                source = x - step_x
                halo = side_row(recv_c, recv_d, i, first + source, planes) if step_y else None
                out_v[i, x] = streamed(i, x, rel, rel[i, source], halo)

        def put(x, low, high, out_v=out_v, out_hbm=out_hbm, first=first):
            return pltpu.make_async_copy(
                out_v.at[low:high, x], out_hbm.at[low:high, x], out_sem.at[first + x]
            )

        def inner(x, carry, emit=emit, put=put):
            emit(x, ())
            put(x, 0, 27).start()
            return carry

        lax.fori_loop(1, size_x - 1, inner, 0)
        emit(0, (1,))
        copies.append(put(0, 0, 18))
        copies[-1].start()
        emit(size_x - 1, (-1,))
        copies.append(put(size_x - 1, 9, 27))
        copies[-1].start()
        copies.extend(put(x, 0, 27) for x in range(1, size_x - 1))
    for copy in copies:
        copy.wait()


def middle_kernel(
    main_hbm, cells_in, rates_hbm, rel_old, rel_prec, recv_c, recv_d, recv_a, inlet,
    rel_main, main_out, prec_out,
    main_in, rates_ref, main_v, prec_v, in_sem, rates_sem, out_sem,
):
    @pl.when(lax.axis_index("gx") != 0)
    def inner():
        inner_planes(
            main_hbm, cells_in, rates_hbm, rel_main, main_in, rates_ref, in_sem, rates_sem
        )

    @pl.when(lax.axis_index("gx") == 0)
    def stream():
        stream_planes(
            rel_main, rel_prec, recv_c, recv_d, main_out, prec_out, main_v, prec_v, out_sem
        )


def stream_kernel(
    rel_main, rel_prec, recv_c, recv_d, inlet, main_old, prec_old,
    main_out, prec_out, main_v, prec_v, out_sem,
):
    @pl.when(lax.axis_index("gx") != 0)
    def stream():
        stream_planes(
            rel_main, rel_prec, recv_c, recv_d, main_out, prec_out, main_v, prec_v, out_sem
        )


def patch_side(low_side, rel_main, rel_prec, faces, out_refs, stages, out_sem):
    copies = []
    for lattice in (1, 0):
        rel, out_v = (rel_main, rel_prec)[lattice], stages[lattice]
        x = 0 if low_side else rel.shape[1] - 1
        first = 18 if low_side else 0
        for part in range(9):
            value, halo = faces(lattice, low_side, part)
            out_v[part] = streamed(part + first, x, rel, value, halo)
        copies.append(
            pltpu.make_async_copy(
                out_v, out_refs[lattice].at[first : first + 9, x], out_sem.at[lattice]
            )
        )
        copies[-1].start()
    for copy in copies:
        copy.wait()


def face_row(part):
    step_y, step_z = part // 3 - 1, part % 3 - 1
    return (0 if step_y == 1 else 3) + step_z + 1 if step_y else None


def even_edge_kernel(
    rel_main, rel_prec, recv_a, corner_a, main_old, prec_old,
    main_out, prec_out, main_v, prec_v, out_sem,
):
    odd_x = lax.rem(lax.axis_index("gx"), 2)

    def faces(lattice, low_side, part):
        start, size = ((0, main_v.shape[1]), (main_v.shape[1], prec_v.shape[1]))[lattice]
        row = face_row(part)
        halo = None if row is None else corner_a[lattice, row : row + 1, :]
        return recv_a[part, start : start + size], halo

    for low_side in (True, False):

        @pl.when(odd_x == (1 if low_side else 0))
        def patch(low_side=low_side):
            patch_side(
                low_side, rel_main, rel_prec, faces,
                (main_out, prec_out), (main_v, prec_v), out_sem,
            )


def odd_edge_kernel(
    rel_main, rel_prec, recv_b, recv_c, recv_d, corner_b, inlet, main_old, prec_old,
    main_out, prec_out, main_v, prec_v, out_sem,
):
    extent_x = rel_main.shape[1]
    planes = extent_x + rel_prec.shape[1]
    place_x = lax.axis_index("gx")
    odd_x = lax.rem(place_x, 2)
    at_first, at_last = place_x == 0, place_x == lax.axis_size("gx") - 1

    def faces(lattice, low_side, part):
        row = face_row(part)
        halo = None if row is None else corner_b[9 + lattice, row : row + 1, :]
        if lattice:
            return corner_b[part], halo
        value = recv_b[part]
        if low_side:
            whole = jnp.concatenate([inlet[0, part], inlet[1, part]], axis=0)
            return jnp.where(at_first, whole, value), halo
        value = jnp.where(at_last, rel_main[part, extent_x - 1], value)
        if row is not None:
            own = side_row(recv_c, recv_d, part, extent_x - 1, planes)
            halo = jnp.where(at_last, own, halo)
        return value, halo

    for low_side in (True, False):

        @pl.when(odd_x == (0 if low_side else 1))
        def patch(low_side=low_side):
            patch_side(
                low_side, rel_main, rel_prec, faces,
                (main_out, prec_out), (main_v, prec_v), out_sem,
            )


def shards(prec_pops, main_pops, cell_type, rates):
    _, extent_x, extent_y, depth = main_pops.shape
    _, prec_x, prec_y, _ = prec_pops.shape
    count_x, count_y = lax.axis_size("gx"), lax.axis_size("gy")
    assert count_x % 2 == 0 and count_y % 2 == 0 and extent_y == 2 * prec_y
    planes = extent_x + prec_x
    f32 = jnp.float32
    face = (9, extent_y + prec_y, depth)
    side = (9 * planes + 3, depth)
    side_outlet = (9 * planes + 4 + 9 * prec_y, depth)
    params = pltpu.CompilerParams(vmem_limit_bytes=vmem_bytes)
    dma = pltpu.SemaphoreType.DMA
    main_row, prec_row = (27, extent_x, depth), (27, prec_x, depth)
    cells_in, main_rel, prec_rel, send_a, send_b, send_c, send_d = pl.pallas_call(
        border_kernel,
        out_shape=(
            pltpu.VMEM(cell_type.shape, jnp.int32),
            *(
                pltpu.VMEM(shape, f32)
                for shape in (
                    main_pops.shape, prec_pops.shape,
                    face, (9, extent_y, depth), side_outlet, side,
                )
            ),
        ),
        in_specs=[any_space] * 3 + [smem_space],
        out_specs=(vmem_space,) * 7,
        scratch_shapes=[
            *(
                pltpu.VMEM(shape, f32)
                for shape in (
                    (27, 2, extent_y, depth), prec_pops.shape,
                    main_row, main_row, prec_row, prec_row,
                )
            ),
            dma((3 + prec_x,)), dma((2 * planes,)),
        ],
        compiler_params=params,
        name="border",
    )(in_hbm(main_pops), in_hbm(prec_pops), in_hbm(cell_type), in_hbm(rates))
    long_run = pl.CostEstimate(flops=10**9, bytes_accessed=1, transcendentals=0)
    inner_scratch = [pltpu.VMEM(main_pops.shape, f32), pltpu.SMEM(rates.shape, f32)]
    inner_given = in_hbm(main_pops), in_vmem(cells_in), in_hbm(rates)
    main_rel, send_b = pl.pallas_call(
        first_kernel,
        out_shape=(pltpu.VMEM(main_pops.shape, f32), pltpu.VMEM(send_b.shape, f32)),
        in_specs=[any_space, vmem_space, any_space] + [vmem_space] * 2,
        out_specs=(vmem_space,) * 2,
        scratch_shapes=inner_scratch + [dma((extent_x,)), dma(())],
        input_output_aliases={3: 0, 4: 1},
        cost_estimate=long_run,
        compiler_params=params,
        name="inner_first",
    )(*inner_given, in_vmem(main_rel), in_vmem(send_b))
    prec_rel = in_vmem(prec_rel)

    half = count_y // 2
    base = (count_x - 1) * count_y
    to_inlet = [(base + s, s // 2 + half * (s % 2)) for s in range(count_y)]
    recv_a = in_vmem(lax.ppermute(send_a, "gx", swap_pairs(count_x, 0)))
    across = [p for p in swap_pairs(count_x, 1) if abs(p[0] - p[1]) == 1]
    recv_b = in_vmem(lax.ppermute(send_b, "gx", across))
    recv_c = in_vmem(lax.ppermute(send_c, "gy", swap_pairs(count_y, 0)))
    send_d, pair_send = pl.pallas_call(
        relay_kernel,
        out_shape=(pltpu.VMEM(side, f32), pltpu.VMEM((2, 9, prec_y, depth), f32)),
        in_specs=[vmem_space] * 3,
        out_specs=(vmem_space,) * 2,
        compiler_params=params,
        name="relay",
    )(prec_rel, in_vmem(send_d), recv_c)
    inlet = in_vmem(lax.ppermute(pair_send, ("gx", "gy"), to_inlet))
    fetched = []
    if count_y != 4:
        own_rows = pl.pallas_call(
            own_rows_kernel,
            out_shape=pltpu.VMEM((8, depth), f32),
            in_specs=[vmem_space],
            out_specs=vmem_space,
            compiler_params=params,
            name="outlet_rows",
        )(prec_rel)
        for shift in (-1, 2):
            for start in (0, half):
                pairs = [((2 * j + shift) % count_y, j) for j in range(start, start + half)]
                fetched.append(in_vmem(lax.ppermute(own_rows, "gy", pairs)))
    recv_d = in_vmem(lax.ppermute(send_d, "gy", swap_pairs(count_y, 1)))

    corner = (2, 8, depth)
    corner_a, corner_b = pl.pallas_call(
        corner_kernel,
        out_shape=(pltpu.VMEM(corner, f32), pltpu.VMEM((11, prec_y, depth), f32)),
        in_specs=[vmem_space] * (3 + len(fetched)),
        out_specs=(vmem_space,) * 2,
        compiler_params=params,
        name="corners",
    )(prec_rel, recv_c, recv_d, *fetched)
    corner_a = in_vmem(lax.ppermute(corner_a, "gx", swap_pairs(count_x, 0)))
    corner_b = in_vmem(lax.ppermute(corner_b, "gx", swap_pairs(count_x, 1)))

    outs = (
        jax.ShapeDtypeStruct(main_pops.shape, f32),
        jax.ShapeDtypeStruct(prec_pops.shape, f32),
    )
    stream_scratch = [pltpu.VMEM(main_pops.shape, f32), pltpu.VMEM(prec_pops.shape, f32)]
    main_rel, main_part, prec_part = pl.pallas_call(
        middle_kernel,
        out_shape=(pltpu.VMEM(main_pops.shape, f32), *outs),
        in_specs=[any_space, vmem_space, any_space] + [vmem_space] * 6,
        out_specs=(vmem_space, any_space, any_space),
        scratch_shapes=inner_scratch + stream_scratch
        + [dma((extent_x,)), dma(()), dma((planes,))],
        input_output_aliases={3: 0},
        cost_estimate=long_run,
        compiler_params=params,
        name="middle",
    )(*inner_given, in_vmem(main_rel), prec_rel, recv_c, recv_d, recv_a, inlet)
    main_rel = in_vmem(main_rel)
    main_part, prec_part = pl.pallas_call(
        stream_kernel,
        out_shape=outs,
        in_specs=[vmem_space] * 5 + [any_space] * 2,
        out_specs=(any_space, any_space),
        scratch_shapes=stream_scratch + [dma((planes,))],
        input_output_aliases={5: 0, 6: 1},
        cost_estimate=long_run,
        compiler_params=params,
        name="stream",
    )(main_rel, prec_rel, recv_c, recv_d, inlet, main_part, prec_part)
    def patched(kernel, name, given, outs_so_far):
        return pl.pallas_call(
            kernel,
            out_shape=outs,
            in_specs=[vmem_space] * len(given) + [any_space] * 2,
            out_specs=(any_space, any_space),
            scratch_shapes=[
                pltpu.VMEM((9, extent_y, depth), f32),
                pltpu.VMEM((9, prec_y, depth), f32),
                dma((2,)),
            ],
            input_output_aliases={len(given): 0, len(given) + 1: 1},
            compiler_params=params,
            name=name,
        )(*given, *outs_so_far)

    even_given = main_rel, prec_rel, recv_a, corner_a
    odd_given = main_rel, prec_rel, recv_b, recv_c, recv_d, corner_b, inlet
    partial = patched(even_edge_kernel, "even_edges", even_given, (main_part, prec_part))
    main_next, prec_next = patched(odd_edge_kernel, "odd_edges", odd_given, partial)
    return prec_next, main_next


def solution(mesh):
    placed = (P(None, "gx", "gy", None), P(None, "gx", "gy", None), P("gx", "gy", None), P())
    return jax.shard_map(
        shards,
        mesh=mesh,
        in_specs=placed,
        out_specs=(P(None, "gx", "gy", None), P(None, "gx", "gy", None)),
        check_vma=False,
    )
```

```python
import functools

import jax
import jax.numpy as jnp
import numpy as np
from jax import lax
from jax.experimental import pallas as pl
from jax.experimental.pallas import tpu as pltpu
from jax.sharding import PartitionSpec as P

drag_scale = -0.5 * 0.75
vmem_bytes = 24 * 1024 * 1024
any_space = pl.BlockSpec(memory_space=pltpu.HBM)
vmem_space = pl.BlockSpec(memory_space=pltpu.VMEM)
smem_space = pl.BlockSpec(memory_space=pltpu.SMEM)


def in_vmem(value):
    return pltpu.with_memory_space_constraint(value, pltpu.VMEM)


def in_hbm(value):
    return pltpu.with_memory_space_constraint(value, pltpu.HBM)


def swap_pairs(count, first):
    pairs = [(i, (i + 1) % count) for i in range(first, count, 2)]
    return [p for a, b in pairs for p in ((a, b), (b, a))]


def along_axes(values, stride, step):
    out = list(values)
    for start in range(27):
        if (start // stride) % 3 == 0:
            where = (start, start + stride, start + 2 * stride)
            for place, value in zip(where, step(*(values[i] for i in where))):
                out[place] = value
    return out


def to_moments(low, mid, high):
    outer = low + high
    return outer + mid, high - low, outer


def from_moments(zeroth, first, second):
    low, high = second - first, second + first
    return low, zeroth - (low + high), high


def digits(k):
    return k // 9, k // 3 % 3, k % 3


def moment_scales(rates_ref):
    keep, pull = [], []
    for k in range(27):
        ones = digits(k).count(1)
        twos = digits(k).count(2)
        half = 0.5 ** (ones + twos)
        third = 3.0 ** -(twos if ones else max(twos - 1, 0))
        rate = rates_ref[k]
        keep.append((1.0 - rate) * half)
        pull.append(rate * (half * third))
    return keep, pull


def relaxed_tile(pops, keep, pull, disk):
    m = pops
    for stride in (1, 3, 9):
        m = along_axes(m, stride, to_moments)
    density, flux = m[0], (m[9], m[3], m[1])
    inverse = 1.0 / density
    speed = [f * inverse for f in flux]
    third = density * (1.0 / 3.0)
    product = {(a, b): flux[a] * speed[b] for a in range(3) for b in range(a, 3)}
    drag = None
    if disk is not None:
        drag = jnp.where(disk, drag_scale * flux[0] * jnp.abs(speed[0]), 0.0)
    target = []
    for k in range(27):
        ones = [a for a in range(3) if digits(k)[a] == 1]
        twos = [a for a in range(3) if digits(k)[a] == 2]
        half = 0.5 ** (len(ones) + len(twos))
        if not ones and not twos:
            value = density
        elif len(ones) == 1 and not twos:
            value = m[k] * half
        elif len(ones) == 3:
            value = m[k] * keep[k]
        else:
            if len(ones) == 1:
                pulled = flux[ones[0]]
            elif len(ones) == 2:
                pulled = product[tuple(ones)]
            else:
                pulled = third
                for a in twos:
                    pulled = pulled + product[a, a]
            value = m[k] * keep[k] + pulled * pull[k]
        if drag is not None and ones == [0]:
            value = value + drag * (half * 3.0 ** -len(twos))
        target.append(value)
    for stride in (9, 3, 1):
        target = along_axes(target, stride, from_moments)
    return target


def main_plane(main_in, cells_in, rel_main, keep, pull, slot, x):
    extent_y, depth = main_in.shape[2:]
    for y in range(0, extent_y, 8):
        for z in range(0, depth, 128):
            rows, lanes = pl.ds(y, 8), pl.ds(z, 128)
            kind = cells_in[x, rows, lanes]
            pops = [main_in[i, slot, rows, lanes] for i in range(27)]
            relaxed = relaxed_tile(pops, keep, pull, kind == 2)
            for i in range(27):
                value = relaxed[i]
                if z == 0:
                    value = jnp.where(kind == 1, pops[26 - i], value)
                rel_main[i, x, rows, lanes] = value


def border_kernel(
    main_hbm, prec_hbm, cells_hbm, rates_ref,
    cells_in, rel_main, rel_prec, send_a, send_b, send_c, send_d,
    outer_in, prec_in, main_low, main_high, prec_low, prec_high, plane_sem, row_sem,
):
    extent_x, extent_y, depth = rel_main.shape[1:]
    prec_x, prec_y = prec_in.shape[1:3]
    planes = extent_x + prec_x
    odd_x = lax.rem(lax.axis_index("gx"), 2)
    odd_y = lax.rem(lax.axis_index("gy"), 2)

    def pick(odd, even_value, odd_value):
        return jnp.where(odd == 0, even_value, odd_value)

    def fetch_prec(x):
        return pltpu.make_async_copy(prec_hbm.at[:, x], prec_in.at[:, x], plane_sem.at[3 + x])

    def fetch_outer(k):
        x = k * (extent_x - 1)
        return pltpu.make_async_copy(main_hbm.at[:, x], outer_in.at[:, k], plane_sem.at[k])

    fetch_cells = pltpu.make_async_copy(cells_hbm, cells_in, plane_sem.at[2])
    rows = []
    for hbm, low, high in ((main_hbm, main_low, main_high), (prec_hbm, prec_low, prec_high)):
        for x in range(hbm.shape[1]):
            for y, to in ((0, low), (hbm.shape[2] - 1, high)):
                rows.append(
                    pltpu.make_async_copy(
                        hbm.at[:, x, pl.ds(y, 1), :], to.at[:, pl.ds(x, 1), :],
                        row_sem.at[len(rows)],
                    )
                )
    for x in range(prec_x):
        fetch_prec(x).start()
    fetch_cells.start()
    for k in range(2):
        fetch_outer(k).start()
    for copy in rows:
        copy.start()
    keep, pull = moment_scales(rates_ref)

    def prec_plane(x, carry):
        fetch_prec(x).wait()
        for y in range(0, prec_y, 8):
            for z in range(0, depth, 128):
                rows, lanes = pl.ds(y, 8), pl.ds(z, 128)
                pops = [prec_in[i, x, rows, lanes] for i in range(27)]
                for i, value in enumerate(relaxed_tile(pops, keep, pull, None)):
                    rel_prec[i, x, rows, lanes] = value
        return carry

    def outer_plane(k, carry):
        fetch_outer(k).wait()
        main_plane(outer_in, cells_in, rel_main, keep, pull, k, k * (extent_x - 1))
        return carry

    lax.fori_loop(0, prec_x, prec_plane, 0)
    fetch_cells.wait()
    lax.fori_loop(0, 2, outer_plane, 0)

    for rel, first, size_x, size_y in (
        (rel_main, 0, extent_x, extent_y),
        (rel_prec, extent_y, prec_x, prec_y),
    ):
        for i in range(9):
            high, low = rel[18 + i, size_x - 1], rel[i, 0]
            send_a[i, first : first + size_y] = pick(odd_x, high, low)
            if first == 0:
                send_b[i] = pick(odd_x, low, high)
    for i in range(9):
        send_c[pl.ds(9 * planes + 4 + i * prec_y, prec_y), :] = rel_prec[18 + i, prec_x - 1]
    for step in range(3):
        place = pl.ds(9 * planes + step, 1)
        first, last = outlet_rows(rel_prec, step)
        send_c[place, :] = pick(odd_y, first, last)

    for copy in rows:
        copy.wait()
    for z in range(0, depth, 128):
        lanes = pl.ds(z, 128)
        for first, size_x, ends in (
            (0, extent_x, ((main_low, 0), (main_high, extent_y - 1))),
            (extent_x, prec_x, ((prec_low, None), (prec_high, None))),
        ):
            found = []
            for ref, y in ends:
                pops = [ref[i, :, lanes] for i in range(27)]
                kind = None if y is None else cells_in[:, y, lanes]
                disk = None if y is None else kind == 2
                relaxed = relaxed_tile(pops, keep, pull, disk)
                if y is not None and z == 0:
                    relaxed = [
                        jnp.where(kind == 1, pops[26 - i], relaxed[i]) for i in range(27)
                    ]
                found.append(relaxed)
            for pair in range(9):
                down, up = 9 * (pair // 3) + pair % 3, 9 * (pair // 3) + 6 + pair % 3
                place = pl.ds(pair * planes + first, size_x)
                low, high = found[0][down], found[1][up]
                send_c[place, lanes] = pick(odd_y, high, low)
                send_d[place, lanes] = pick(odd_y, low, high)


def inner_planes(
    main_hbm, cells_in, rates_hbm, rel_main, main_in, rates_ref, in_sem, rates_sem
):
    def fetch(x):
        return pltpu.make_async_copy(main_hbm.at[:, x], main_in.at[:, x], in_sem.at[x])

    extent_x = main_in.shape[1]
    fetch_rates = pltpu.make_async_copy(rates_hbm, rates_ref, rates_sem)
    fetch_rates.start()
    for x in range(1, extent_x - 1):
        fetch(x).start()
    fetch_rates.wait()
    keep, pull = moment_scales(rates_ref)

    def plane(x, carry):
        fetch(x).wait()
        main_plane(main_in, cells_in, rel_main, keep, pull, x, x)
        return carry

    lax.fori_loop(1, extent_x - 1, plane, 0)


def first_kernel(
    main_hbm, cells_in, rates_hbm, rel_old, held_old,
    rel_main, held, main_in, rates_ref, in_sem, rates_sem,
):
    @pl.when(lax.axis_index("gx") == 0)
    def inner():
        inner_planes(
            main_hbm, cells_in, rates_hbm, rel_main, main_in, rates_ref, in_sem, rates_sem
        )


def outlet_rows(rel_prec, step):
    prec_x, prec_y = rel_prec.shape[1:3]
    first = rel_prec[18 + step, prec_x - 1, 0:1, :]
    return first, rel_prec[24 + step, prec_x - 1, prec_y - 1 : prec_y, :]


def relay_kernel(rel_prec, send_d, recv_c, relayed_d, pair_send):
    prec_x, prec_y = rel_prec.shape[1:3]
    own = send_d.shape[0] // 9 * 9
    relayed_d[0:own] = send_d[0:own]
    for step in range(send_d.shape[0] - own):
        place = pl.ds(own + step, 1)
        relayed_d[place, :] = recv_c[place, :]
    odd_y = lax.rem(lax.axis_index("gy"), 2)
    for i in range(9):
        mine = rel_prec[18 + i, prec_x - 1]
        other = recv_c[pl.ds(own + 4 + i * prec_y, prec_y), :]
        pair_send[0, i] = jnp.where(odd_y == 0, mine, other)
        pair_send[1, i] = jnp.where(odd_y == 0, other, mine)


def own_rows_kernel(rel_prec, own_rows):
    own_rows[...] = jnp.zeros_like(own_rows)
    for step in range(3):
        first, last = outlet_rows(rel_prec, step)
        own_rows[step : step + 1, :] = last
        own_rows[3 + step : 4 + step, :] = first


def side_rows(recv_c, recv_d, odd_y, place):
    one, other = recv_c[pl.ds(place, 1), :], recv_d[pl.ds(place, 1), :]
    return jnp.where(odd_y == 0, other, one), jnp.where(odd_y == 0, one, other)


def corner_kernel(rel_prec, recv_c, recv_d, *rest):
    fetched, (corner_a, corner_b) = rest[:-2], rest[-2:]
    prec_x, prec_y = rel_prec.shape[1:3]
    planes = recv_d.shape[0] // 9
    extent_x = planes - prec_x
    place_x, place_y = lax.axis_index("gx"), lax.axis_index("gy")
    count_y = lax.axis_size("gy")
    odd_x, odd_y = lax.rem(place_x, 2), lax.rem(place_y, 2)
    at_last = place_x == lax.axis_size("gx") - 1

    def inlet_rows(step, low, high):
        if fetched:
            near = place_y < count_y // 2
            last = jnp.where(
                near, fetched[0][step : step + 1, :], fetched[1][step : step + 1, :]
            )
            first = jnp.where(
                near, fetched[2][3 + step : 4 + step, :], fetched[3][3 + step : 4 + step, :]
            )
            return last, first
        own_first, own_last = outlet_rows(rel_prec, step)
        beside = recv_c[pl.ds(9 * planes + step, 1), :]
        beyond = recv_d[pl.ds(9 * planes + step, 1), :]

        def choose(*options):
            value = options[0]
            for k in range(1, 4):
                value = jnp.where(place_y == k, options[k], value)
            return value

        return choose(low, own_last, beside, beyond), choose(beyond, beside, own_first, high)

    corner_a[...] = jnp.zeros_like(corner_a)
    for i in range(9):
        corner_b[i] = jnp.where(odd_x == 0, rel_prec[i, 0], rel_prec[18 + i, prec_x - 1])
    corner_b[9:11] = jnp.zeros((2,) + corner_b.shape[1:], jnp.float32)
    for step in range(3):
        outlet = side_rows(recv_c, recv_d, odd_y, (6 + step) * planes + planes - 1)
        inlet = inlet_rows(step, outlet[0], outlet[1])
        for lattice, (x_low, x_high) in enumerate(
            ((0, extent_x - 1), (extent_x, planes - 1))
        ):
            lows = side_rows(recv_c, recv_d, odd_y, step * planes + x_low)
            highs = side_rows(recv_c, recv_d, odd_y, (6 + step) * planes + x_high)
            for k in range(2):
                place = pl.ds(3 * k + step, 1)
                low, high = lows[k], highs[k]
                corner_a[lattice, place, :] = jnp.where(odd_x == 0, high, low)
                value = jnp.where(odd_x == 0, low, high)
                if lattice == 0:
                    value = jnp.where(at_last, inlet[k], value)
                corner_b[9 + lattice, place, :] = value


def streamed(i, x, rel, source_rows, halo_row):
    size_y, depth = rel.shape[2:]
    _, step_y, step_z = (d - 1 for d in digits(i))
    value = source_rows
    if step_y:
        row = lax.broadcasted_iota(jnp.int32, (size_y, depth), 0)
        value = pltpu.roll(value, 1 if step_y == 1 else size_y - 1, 0)
        value = jnp.where(row == (0 if step_y == 1 else size_y - 1), halo_row, value)
    if step_z:
        lane = lax.broadcasted_iota(jnp.int32, (size_y, depth), 1)
        value = pltpu.roll(value, 1 if step_z == 1 else depth - 1, 1)
        value = jnp.where(lane == (0 if step_z == 1 else depth - 1), rel[26 - i, x], value)
    return value


def side_row(recv_c, recv_d, i, place, planes):
    step_x, step_y, step_z = (d - 1 for d in digits(i))
    odd = lax.rem(lax.axis_index("gy"), 2)
    where = pl.ds((3 * (step_x + 1) + step_z + 1) * planes + place, 1)
    from_low = odd if step_y == 1 else 1 - odd
    return jnp.where(from_low == 1, recv_c[where, :], recv_d[where, :])


def stream_planes(
    rel_main, rel_prec, recv_c, recv_d, main_out, prec_out, main_v, prec_v, out_sem,
):
    planes = rel_main.shape[1] + rel_prec.shape[1]
    copies = []
    for rel, out_v, out_hbm, first in (
        (rel_main, main_v, main_out, 0),
        (rel_prec, prec_v, prec_out, rel_main.shape[1]),
    ):
        size_x = rel.shape[1]

        def emit(x, edges, rel=rel, out_v=out_v, first=first):
            for i in range(27):
                step_x, step_y, _ = (d - 1 for d in digits(i))
                if step_x in edges:
                    continue
                source = x - step_x
                halo = side_row(recv_c, recv_d, i, first + source, planes) if step_y else None
                out_v[i, x] = streamed(i, x, rel, rel[i, source], halo)

        def put(x, low, high, out_v=out_v, out_hbm=out_hbm, first=first):
            return pltpu.make_async_copy(
                out_v.at[low:high, x], out_hbm.at[low:high, x], out_sem.at[first + x]
            )

        def inner(x, carry, emit=emit, put=put):
            emit(x, ())
            put(x, 0, 27).start()
            return carry

        lax.fori_loop(1, size_x - 1, inner, 0)
        emit(0, (1,))
        copies.append(put(0, 0, 18))
        copies[-1].start()
        emit(size_x - 1, (-1,))
        copies.append(put(size_x - 1, 9, 27))
        copies[-1].start()
        copies.extend(put(x, 0, 27) for x in range(1, size_x - 1))
    for copy in copies:
        copy.wait()


def middle_kernel(
    main_hbm, cells_in, rates_hbm, rel_old, rel_prec, recv_c, recv_d, recv_a, inlet,
    rel_main, main_out, prec_out,
    main_in, rates_ref, main_v, prec_v, in_sem, rates_sem, out_sem,
):
    @pl.when(lax.axis_index("gx") != 0)
    def inner():
        inner_planes(
            main_hbm, cells_in, rates_hbm, rel_main, main_in, rates_ref, in_sem, rates_sem
        )

    @pl.when(lax.axis_index("gx") == 0)
    def stream():
        stream_planes(
            rel_main, rel_prec, recv_c, recv_d, main_out, prec_out, main_v, prec_v, out_sem
        )


def stream_kernel(
    rel_main, rel_prec, recv_c, recv_d, inlet, main_old, prec_old,
    main_out, prec_out, main_v, prec_v, out_sem,
):
    @pl.when(lax.axis_index("gx") != 0)
    def stream():
        stream_planes(
            rel_main, rel_prec, recv_c, recv_d, main_out, prec_out, main_v, prec_v, out_sem
        )


def edge_kernel(
    rel_main, rel_prec, recv_a, recv_b, recv_c, recv_d, corner_a, corner_b, inlet,
    main_old, prec_old, main_out, prec_out, main_v, prec_v, out_sem,
):
    extent_x, extent_y, _ = rel_main.shape[1:]
    prec_x, prec_y = rel_prec.shape[1:3]
    planes = extent_x + prec_x
    place_x, place_y = lax.axis_index("gx"), lax.axis_index("gy")
    count_x, count_y = lax.axis_size("gx"), lax.axis_size("gy")
    odd_x = lax.rem(place_x, 2)
    at_first, at_last = place_x == 0, place_x == count_x - 1
    copies = []
    for rel, out_v, out_hbm, lattice in (
        (rel_prec, prec_v, prec_out, 1),
        (rel_main, main_v, main_out, 0),
    ):
        size_x, size_y = rel.shape[1:3]
        start_y = extent_y if lattice else 0
        for low_side in (True, False):
            x = 0 if low_side else size_x - 1
            from_one = odd_x if low_side else 1 - odd_x
            for part in range(9):
                i = part + (18 if low_side else 0)
                step_y, step_z = digits(i)[1] - 1, digits(i)[2] - 1
                rows = pl.ds(start_y, size_y)
                other = corner_b[part] if lattice else recv_b[part]
                value = jnp.where(from_one == 1, recv_a[part, rows], other)
                halo = None
                if step_y:
                    where = pl.ds((0 if step_y == 1 else 3) + step_z + 1, 1)
                    halo = jnp.where(
                        from_one == 1, corner_a[lattice, where, :], corner_b[9 + lattice, where, :]
                    )
                if not lattice and low_side:
                    whole = jnp.concatenate([inlet[0, part], inlet[1, part]], axis=0)
                    value = jnp.where(at_first, whole, value)
                if not lattice and not low_side:
                    value = jnp.where(at_last, rel[i, size_x - 1], value)
                    if step_y:
                        row = side_row(recv_c, recv_d, i, size_x - 1, planes)
                        halo = jnp.where(at_last, row, halo)
                out_v[part, 0 if low_side else 1] = streamed(i, x, rel, value, halo)
            first = 18 if low_side else 0
            copy = pltpu.make_async_copy(
                out_v.at[:, 0 if low_side else 1],
                out_hbm.at[first : first + 9, x],
                out_sem.at[2 * lattice + (0 if low_side else 1)],
            )
            copy.start()
            copies.append(copy)
    for copy in copies:
        copy.wait()


def shards(prec_pops, main_pops, cell_type, rates):
    _, extent_x, extent_y, depth = main_pops.shape
    _, prec_x, prec_y, _ = prec_pops.shape
    count_x, count_y = lax.axis_size("gx"), lax.axis_size("gy")
    assert count_x % 2 == 0 and count_y % 2 == 0 and extent_y == 2 * prec_y
    planes = extent_x + prec_x
    f32 = jnp.float32
    face = (9, extent_y + prec_y, depth)
    side = (9 * planes + 3, depth)
    side_outlet = (9 * planes + 4 + 9 * prec_y, depth)
    params = pltpu.CompilerParams(vmem_limit_bytes=vmem_bytes)
    dma = pltpu.SemaphoreType.DMA
    main_row, prec_row = (27, extent_x, depth), (27, prec_x, depth)
    cells_in, main_rel, prec_rel, send_a, send_b, send_c, send_d = pl.pallas_call(
        border_kernel,
        out_shape=(
            pltpu.VMEM(cell_type.shape, jnp.int32),
            *(
                pltpu.VMEM(shape, f32)
                for shape in (
                    main_pops.shape, prec_pops.shape,
                    face, (9, extent_y, depth), side_outlet, side,
                )
            ),
        ),
        in_specs=[any_space] * 3 + [smem_space],
        out_specs=(vmem_space,) * 7,
        scratch_shapes=[
            *(
                pltpu.VMEM(shape, f32)
                for shape in (
                    (27, 2, extent_y, depth), prec_pops.shape,
                    main_row, main_row, prec_row, prec_row,
                )
            ),
            dma((3 + prec_x,)), dma((2 * planes,)),
        ],
        compiler_params=params,
        name="border",
    )(in_hbm(main_pops), in_hbm(prec_pops), in_hbm(cell_type), in_hbm(rates))
    long_run = pl.CostEstimate(flops=10**9, bytes_accessed=1, transcendentals=0)
    inner_scratch = [pltpu.VMEM(main_pops.shape, f32), pltpu.SMEM(rates.shape, f32)]
    inner_given = in_hbm(main_pops), in_vmem(cells_in), in_hbm(rates)
    main_rel, send_b = pl.pallas_call(
        first_kernel,
        out_shape=(pltpu.VMEM(main_pops.shape, f32), pltpu.VMEM(send_b.shape, f32)),
        in_specs=[any_space, vmem_space, any_space] + [vmem_space] * 2,
        out_specs=(vmem_space,) * 2,
        scratch_shapes=inner_scratch + [dma((extent_x,)), dma(())],
        input_output_aliases={3: 0, 4: 1},
        cost_estimate=long_run,
        compiler_params=params,
        name="inner_first",
    )(*inner_given, in_vmem(main_rel), in_vmem(send_b))
    prec_rel = in_vmem(prec_rel)

    half = count_y // 2
    base = (count_x - 1) * count_y
    to_inlet = [(base + s, s // 2 + half * (s % 2)) for s in range(count_y)]
    recv_a = in_vmem(lax.ppermute(send_a, "gx", swap_pairs(count_x, 0)))
    across = [p for p in swap_pairs(count_x, 1) if abs(p[0] - p[1]) == 1]
    recv_b = in_vmem(lax.ppermute(send_b, "gx", across))
    recv_c = in_vmem(lax.ppermute(send_c, "gy", swap_pairs(count_y, 0)))
    send_d, pair_send = pl.pallas_call(
        relay_kernel,
        out_shape=(pltpu.VMEM(side, f32), pltpu.VMEM((2, 9, prec_y, depth), f32)),
        in_specs=[vmem_space] * 3,
        out_specs=(vmem_space,) * 2,
        compiler_params=params,
        name="relay",
    )(prec_rel, in_vmem(send_d), recv_c)
    inlet = in_vmem(lax.ppermute(pair_send, ("gx", "gy"), to_inlet))
    fetched = []
    if count_y != 4:
        own_rows = pl.pallas_call(
            own_rows_kernel,
            out_shape=pltpu.VMEM((8, depth), f32),
            in_specs=[vmem_space],
            out_specs=vmem_space,
            compiler_params=params,
            name="outlet_rows",
        )(prec_rel)
        for shift in (-1, 2):
            for start in (0, half):
                pairs = [((2 * j + shift) % count_y, j) for j in range(start, start + half)]
                fetched.append(in_vmem(lax.ppermute(own_rows, "gy", pairs)))
    recv_d = in_vmem(lax.ppermute(send_d, "gy", swap_pairs(count_y, 1)))

    corner = (2, 8, depth)
    corner_a, corner_b = pl.pallas_call(
        corner_kernel,
        out_shape=(pltpu.VMEM(corner, f32), pltpu.VMEM((11, prec_y, depth), f32)),
        in_specs=[vmem_space] * (3 + len(fetched)),
        out_specs=(vmem_space,) * 2,
        compiler_params=params,
        name="corners",
    )(prec_rel, recv_c, recv_d, *fetched)
    corner_a = in_vmem(lax.ppermute(corner_a, "gx", swap_pairs(count_x, 0)))
    corner_b = in_vmem(lax.ppermute(corner_b, "gx", swap_pairs(count_x, 1)))

    outs = (
        jax.ShapeDtypeStruct(main_pops.shape, f32),
        jax.ShapeDtypeStruct(prec_pops.shape, f32),
    )
    stream_scratch = [pltpu.VMEM(main_pops.shape, f32), pltpu.VMEM(prec_pops.shape, f32)]
    main_rel, main_part, prec_part = pl.pallas_call(
        middle_kernel,
        out_shape=(pltpu.VMEM(main_pops.shape, f32), *outs),
        in_specs=[any_space, vmem_space, any_space] + [vmem_space] * 6,
        out_specs=(vmem_space, any_space, any_space),
        scratch_shapes=inner_scratch + stream_scratch
        + [dma((extent_x,)), dma(()), dma((planes,))],
        input_output_aliases={3: 0},
        cost_estimate=long_run,
        compiler_params=params,
        name="middle",
    )(*inner_given, in_vmem(main_rel), prec_rel, recv_c, recv_d, recv_a, inlet)
    main_rel = in_vmem(main_rel)
    main_part, prec_part = pl.pallas_call(
        stream_kernel,
        out_shape=outs,
        in_specs=[vmem_space] * 5 + [any_space] * 2,
        out_specs=(any_space, any_space),
        scratch_shapes=stream_scratch + [dma((planes,))],
        input_output_aliases={5: 0, 6: 1},
        cost_estimate=long_run,
        compiler_params=params,
        name="stream",
    )(main_rel, prec_rel, recv_c, recv_d, inlet, main_part, prec_part)
    main_next, prec_next = pl.pallas_call(
        edge_kernel,
        out_shape=outs,
        in_specs=[vmem_space] * 9 + [any_space] * 2,
        out_specs=(any_space, any_space),
        scratch_shapes=[
            pltpu.VMEM((9, 2, extent_y, depth), f32),
            pltpu.VMEM((9, 2, prec_y, depth), f32),
            dma((4,)),
        ],
        input_output_aliases={9: 0, 10: 1},
        compiler_params=params,
        name="edges",
    )(
        main_rel, prec_rel, recv_a, recv_b, recv_c, recv_d,
        corner_a, corner_b, inlet, main_part, prec_part,
    )
    return prec_next, main_next


def solution(mesh):
    placed = (P(None, "gx", "gy", None), P(None, "gx", "gy", None), P("gx", "gy", None), P())
    return jax.shard_map(
        shards,
        mesh=mesh,
        in_specs=placed,
        out_specs=(P(None, "gx", "gy", None), P(None, "gx", "gy", None)),
        check_vma=False,
    )
```
